256 devices in a mesh: head: 8 (over z_hi, core), frame: 32 (over z_lo, y, x).
Axes of the slice: x: 4, y: 4, z: 8 (z_hi: 4, z_lo: 2; z = z_hi * 2 + z_lo), core: 2. Of those that a mesh axis runs over, the one named last changes fastest.
Arguments:
- resid: bfloat16 [12288, 5120], P('frame'), may hold values from -6 to 6
- qkv: bfloat16 [12288, 3, 5120], P(('frame', 'head')), may hold values from -12 to 12
- band: int32 [32, 9], P('frame'), may hold values from 1 to 384, as said below
- out_weight: bfloat16 [5120, 5120], P('head'), may hold values from -0.078125 to 0.078125
- modulation: float32 [4, 5120], replicated, may hold values from -3 to 3
- up_weight: bfloat16 [5120, 6912], P('frame', 'head'), may hold values from -0.078125 to 0.078125
- down_weight: bfloat16 [6912, 5120], P('head', 'frame'), may hold values from -0.078125 to 0.078125
Outputs:
- mixed: bfloat16 [12288, 5120], P(('frame', 'head'))
The draws below stay inside these ranges and needn't reach their ends.
Inputs may be any that keep to these rules, and one draw needn't show every extreme that they name: `band`: column 0 (the block itself) is 384; the column of a partner at distance d is at most 384 // d.
All inputs are finite; a program needn't handle non-finite values.
Results may differ from the reference program's by a relative error of at most 0.012.
Values may be sent and summed in bfloat16 or wider, within the bound.
A program may use at most 128 MiB of HBM per device.

```python
import math
import jax
import jax.numpy as jnp
from jax import lax

D = 5120
FF = 6912
HEADS = 40
HD = 128
SLOTS = 9
BLOCK = 384
NBLK = 32
SEQ = 12288
INNER = 5120
N_HEAD = 8


def partner_rows():
    rows = jnp.arange(SEQ, dtype=jnp.int32)
    position = rows % BLOCK
    code = position % 16
    planted = code < 8
    offset_table = jnp.array([-8, -4, -2, -1, 1, 2, 4, 8], jnp.int32)
    shift = offset_table[code % 8]
    source = (rows - shift * BLOCK) % SEQ
    return (planted, source.astype(jnp.int32))


def draw_qkv(key, part):
    key = jax.random.fold_in(key, 11)
    base_key = jax.random.fold_in(key, 0)
    align_key = jax.random.fold_in(key, 2)
    size_key = jax.random.fold_in(key, 3)
    planted, source = partner_rows()
    entries = jnp.clip(jax.random.normal(base_key, (SEQ, 3, HEADS * HD), jnp.float32), -4.0, 4.0)
    strength = jax.random.uniform(size_key, (SEQ,), jnp.float32, 1.5, 2.2)
    shared = jnp.clip(jax.random.normal(align_key, (SEQ, HEADS * HD), jnp.float32), -3.0, 3.0)
    aligned = strength[:, None] * shared
    partner_copy = aligned[source]
    query_part = jnp.where(planted[:, None], aligned, entries[:, 0])
    key_part = jnp.where(planted[:, None], partner_copy, entries[:, 1])
    entries = jnp.stack([query_part, key_part, entries[:, 2]], 1)
    return entries.astype(jnp.bfloat16)


def draw_band(key, part):
    key = jax.random.fold_in(key, 12)
    distance = jnp.array([1, 8, 4, 2, 1, 1, 2, 4, 8], jnp.int32)
    limit = BLOCK // distance
    widths = jax.random.randint(key, (NBLK, SLOTS), 1, limit[None, :] + 1, dtype=jnp.int32)
    slot_index = jnp.arange(SLOTS, dtype=jnp.int32)
    widths = jnp.where(slot_index[None, :] == 0, BLOCK, widths)
    return widths.astype(jnp.int32)


def level_of(own_key, extent, cuts, smallest, largest):
    level = 1.0
    for axis_at, parts in cuts:
        draws = jax.random.uniform(jax.random.fold_in(jax.random.fold_in(own_key, 6), axis_at), (parts,), jnp.float32, smallest / len(cuts), largest / len(cuts))
        level = level * jnp.repeat(jnp.exp(draws), extent[axis_at] // parts).reshape((-1,) + (1,) * (len(extent) - 1 - axis_at))
    return level


def bell_draw(stream_key, extent, deviation, most, shards=(), kind=jnp.bfloat16):
    values = deviation * jax.random.normal(stream_key, extent, jnp.float32)
    if shards:
        values = values * level_of(stream_key, extent, shards, -0.22, 0.18)
    return jnp.clip(values, -most, most).astype(kind)


def setup_inputs(seed: int = 0) -> dict:
    splits = jax.random.split(jax.random.key(seed), 8)
    return {
        "resid": bell_draw(splits[0], (SEQ, D), 1.0, 6.0, ((0, 32),)),
        "qkv": draw_qkv(jax.random.fold_in(splits[7], 71), 0),
        "band": draw_band(jax.random.fold_in(splits[7], 71), 0),
        "out_weight": bell_draw(splits[3], (INNER, D), INNER ** -0.5, 0.078125, ((0, 8),)),
        "modulation": bell_draw(splits[4], (4, D), 0.5, 3.0, (), jnp.float32),
        "up_weight": bell_draw(splits[5], (D, FF), D ** -0.5, 0.078125, ((0, 32), (1, 8))),
        "down_weight": bell_draw(splits[6], (FF, D), FF ** -0.5, 0.078125, ((0, 8), (1, 32))),
    }


partner_offsets = (0, -8, -4, -2, -1, 1, 2, 4, 8)

def rounded(values):
    narrow = lax.optimization_barrier(values.astype(jnp.bfloat16))
    return narrow.astype(jnp.float32)

def modulate(residual_state, shift_row, scale_row):
    average = lax.optimization_barrier(jnp.mean(residual_state, axis=-1, keepdims=True))
    centered = residual_state - average
    variance = lax.optimization_barrier(jnp.mean(centered * centered, axis=-1, keepdims=True))
    normal_form = centered * lax.rsqrt(variance + 1e-06)
    return (normal_form * (1.0 + scale_row) + shift_row).astype(jnp.bfloat16)

def attend_block(queries, key_rows, value_rows, band, block_index):
    score_scale = 1.0 / math.sqrt(HD)
    first_row = (block_index * BLOCK).astype(jnp.int32)
    query_block = lax.dynamic_slice_in_dim(queries, first_row, BLOCK, 0).astype(jnp.float32)
    offsets = jnp.array(partner_offsets, jnp.int32)
    partner = block_index + offsets
    present = (partner >= 0) & (partner < NBLK)
    clipped = jnp.clip(partner, 0, NBLK - 1).astype(jnp.int32)
    key_block = jnp.stack([lax.dynamic_slice_in_dim(key_rows, (clipped[slot] * BLOCK).astype(jnp.int32), BLOCK, 0) for slot in range(SLOTS)], 0).astype(jnp.float32)
    value_block = jnp.stack([lax.dynamic_slice_in_dim(value_rows, (clipped[slot] * BLOCK).astype(jnp.int32), BLOCK, 0) for slot in range(SLOTS)], 0).astype(jnp.float32)
    widths = lax.dynamic_index_in_dim(band, block_index, 0, keepdims=False)
    scores = jnp.einsum('ihd,sjhd->hisj', query_block, key_block) * score_scale
    positions = jnp.arange(BLOCK, dtype=jnp.int32)
    distance = jnp.abs(positions[:, None] - positions[None, :])
    allowed = (distance[None, :, :] < widths[:, None, None]) & present[:, None, None]
    allowed = jnp.transpose(allowed, (1, 0, 2))[None]
    masked = jnp.where(allowed, scores, -1e+30)
    row_max = lax.optimization_barrier(jnp.max(masked, axis=(2, 3), keepdims=True))
    weights = jnp.where(allowed, jnp.exp(masked - row_max), 0.0)
    denominator = lax.optimization_barrier(jnp.sum(weights, axis=(2, 3)))
    probabilities = weights.astype(jnp.bfloat16)
    summed = jnp.einsum('hisj,sjhd->ihd', probabilities.astype(jnp.float32), value_block)
    attended = summed / jnp.transpose(denominator)[:, :, None]
    return attended.astype(jnp.bfloat16).reshape(BLOCK, HEADS * HD)

def reference(resid, qkv, band, out_weight, modulation, up_weight, down_weight):
    queries = qkv[:, 0].reshape(SEQ, HEADS, HD)
    key_rows = qkv[:, 1].reshape(SEQ, HEADS, HD)
    value_rows = qkv[:, 2].reshape(SEQ, HEADS, HD)
    attended = lax.map(lambda block_index: attend_block(queries, key_rows, value_rows, band, block_index), jnp.arange(NBLK, dtype=jnp.int32))
    attended = attended.reshape(SEQ, HEADS * HD)
    head_group = HEADS * HD // N_HEAD
    branch = jnp.zeros((SEQ, D), jnp.float32)
    for group_index in range(N_HEAD):
        lower = group_index * head_group
        partial_value = jnp.dot(attended[:, lower:lower + head_group], out_weight[lower:lower + head_group], preferred_element_type=jnp.float32)
        branch = branch + rounded(partial_value)
    residual_state = resid.astype(jnp.float32) + modulation[0] * branch
    normed = modulate(residual_state, modulation[1], modulation[2])
    unit_group = FF // N_HEAD
    ffn_out = jnp.zeros((SEQ, D), jnp.float32)
    for group_index in range(N_HEAD):
        lower = group_index * unit_group
        projected = jnp.dot(normed, up_weight[:, lower:lower + unit_group], preferred_element_type=jnp.float32)
        hidden = jax.nn.gelu(projected, approximate=True).astype(jnp.bfloat16)
        partial_value = jnp.dot(hidden, down_weight[lower:lower + unit_group], preferred_element_type=jnp.float32)
        ffn_out = ffn_out + rounded(partial_value)
    return (residual_state + modulation[3] * ffn_out).astype(jnp.bfloat16)
```

```python
import functools
import math

import jax
import jax.numpy as jnp
from jax import lax
from jax.experimental import pallas as pl
from jax.experimental.pallas import tpu as pltpu
from jax.sharding import PartitionSpec as P

HD = 128
SLOTS = 9
BLOCK = 384
NBLK = 32
N_HEAD = 8
ROWS = BLOCK // N_HEAD
GROUP = 5
INNER = GROUP * HD
D = 5120
MESH = pl.DeviceIdType.MESH
MIB = 2**20

partner_offsets = (0, -8, -4, -2, -1, 1, 2, 4, 8)
SLOT = {offset: slot for slot, offset in enumerate(partner_offsets)}
QUERY_ROWS = 128
SCALE_LOG2 = math.log2(math.e) / math.sqrt(HD)


def attention_kernel(
    qkv_ref, band_ref, weight_ref, out_ref,
    heads, attended, weight,
    a2a_send, a2a_recv, own_sem, halo_send, halo_recv, weight_sem,
):
    me = lax.axis_index("head")
    block = lax.axis_index("frame")
    x = lax.rem(block, 4)
    row_start = block - x

    def frame_device(frame):
        return {"head": me, "frame": frame}

    def head_device(head):
        return {"head": head, "frame": block}

    barrier = pltpu.get_barrier_semaphore()
    for k in range(1, N_HEAD):
        pl.semaphore_signal(barrier, inc=1, device_id=head_device(lax.rem(me + k, N_HEAD)), device_id_type=MESH)
    for k in range(1, 4):
        pl.semaphore_signal(barrier, inc=1, device_id=frame_device(row_start + lax.rem(x + k, 4)), device_id_type=MESH)
    for k in (4, NBLK - 4):
        pl.semaphore_signal(barrier, inc=1, device_id=frame_device(lax.rem(block + k, NBLK)), device_id_type=MESH)
    pl.semaphore_wait(barrier, N_HEAD - 1 + 3 + 2)

    fetch_weight = pltpu.make_async_copy(weight_ref, weight, weight_sem)
    my_rows = pl.ds(pl.multiple_of(me * ROWS, 16), ROWS)

    def to_peer(j, k):
        peer = lax.rem(me + k, N_HEAD)
        columns = pl.ds(pl.multiple_of(peer * INNER + j * HD, HD), HD)
        return pltpu.make_async_remote_copy(
            qkv_ref.at[:, :, columns], heads.at[j, :, 0, my_rows],
            a2a_send.at[j, k - 1], a2a_recv.at[j, k - 1],
            device_id=head_device(peer), device_id_type=MESH,
        )

    def own_piece(j):
        columns = pl.ds(pl.multiple_of(me * INNER + j * HD, HD), HD)
        return pltpu.make_async_copy(
            qkv_ref.at[:, :, columns], heads.at[j, :, 0, my_rows], own_sem.at[j]
        )

    def send_heads(j, carry):
        for k in (4, 3, 5, 2, 6, 1, 7):
            to_peer(j, k).start()
        own_piece(j).start()
        return carry

    lax.fori_loop(0, GROUP, send_heads, 0)
    fetch_weight.start()

    low4, high4 = block >= 4, block < NBLK - 4
    routes = (
        (1, 0, -4, block + 4, high4),
        (1, 0, 4, block - 4, low4),
        (1, 0, -1, block + 1, x < 3),
        (1, 0, 1, block - 1, x > 0),
        (2, -4, -8, block + 4, low4 & high4),
        (2, 4, 8, block - 4, low4 & high4),
        (2, -4, -1, row_start, (x == 3) & low4),
        (2, 4, 1, row_start + 3, (x == 0) & high4),
        (2, -1, -2, block + 1, (x == 1) | (x == 2)),
        (2, 1, 2, block - 1, (x == 1) | (x == 2)),
        (2, -4, -2, row_start, (x == 2) & low4),
        (2, 4, 2, row_start + 3, (x == 1) & high4),
        (3, -1, -2, block + 1, (x == 0) & low4),
        (3, 1, 2, block - 1, (x == 3) & high4),
    )
    arrivals = (
        (2, -4, low4),
        (2, 4, high4),
        (2, -1, x > 0),
        (2, 1, x < 3),
        (3, -1, (x == 0) & low4),
        (3, 1, (x == 3) & high4),
        (4, -2, block >= 2),
        (4, 2, block < NBLK - 2),
        (4, -8, block >= 8),
        (4, 8, block < NBLK - 8),
    )

    def route_copy(j, index):
        _, source, target, frame, _ = routes[index]
        return pltpu.make_async_remote_copy(
            heads.at[j, 1:3, SLOT[source]], heads.at[j, 1:3, SLOT[target]],
            halo_send.at[j, index], halo_recv.at[j, SLOT[target] - 1],
            device_id=frame_device(jnp.clip(frame, 0, NBLK - 1)), device_id_type=MESH,
        )

    def send_stage(j, stage):
        for index, route in enumerate(routes):
            if route[0] == stage:
                @pl.when(route[4])
                def _():
                    route_copy(j, index).start()

    def wait_stage(j, stage):
        for before, slot, when in arrivals:
            if before == stage:
                @pl.when(when)
                def _():
                    landed = heads.at[j, 1:3, SLOT[slot]]
                    pltpu.make_async_copy(landed, landed, halo_recv.at[j, SLOT[slot] - 1]).wait()

    for offset in partner_offsets[1:]:
        partner = block + offset

        @pl.when((partner < 0) | (partner >= NBLK))
        def _():
            heads[:, 1:3, SLOT[offset]] = jnp.zeros((GROUP, 2, BLOCK, HD), jnp.bfloat16)

    def attend(j):
        widths = []
        for slot, offset in enumerate(partner_offsets):
            partner = block + offset
            present = (partner >= 0) & (partner < NBLK)
            widths.append(jnp.where(present, band_ref[0, slot], 0))
        keys = heads[j, 1].reshape(SLOTS * BLOCK, HD)
        values = heads[j, 2].reshape(SLOTS * BLOCK, HD)
        columns = pl.ds(pl.multiple_of(j * HD, HD), HD)
        for first in range(0, BLOCK, QUERY_ROWS):
            queries = heads[j, 0, 0, first:first + QUERY_ROWS]
            scores = lax.dot_general(
                queries, keys, (((1,), (1,)), ((), ())), preferred_element_type=jnp.float32
            )
            row = lax.broadcasted_iota(jnp.int32, (QUERY_ROWS, BLOCK), 0) + first
            column = lax.broadcasted_iota(jnp.int32, (QUERY_ROWS, BLOCK), 1)
            distance = jnp.abs(row - column)
            parts = []
            for slot in range(SLOTS):
                part = scores[:, slot * BLOCK:(slot + 1) * BLOCK]
                parts.append(jnp.where(distance < widths[slot], part, -1e30))
            top = functools.reduce(jnp.maximum, parts)
            row_max = jnp.max(top, axis=1, keepdims=True)
            weights = [jnp.exp2((part - row_max) * SCALE_LOG2) for part in parts]
            denominator = jnp.sum(functools.reduce(jnp.add, weights), axis=1, keepdims=True)
            probabilities = jnp.concatenate([w.astype(jnp.bfloat16) for w in weights], axis=1)
            summed = jnp.dot(probabilities, values, preferred_element_type=jnp.float32)
            attended[first:first + QUERY_ROWS, columns] = (summed / denominator).astype(jnp.bfloat16)

    def step(it, carry):
        @pl.when(it < GROUP)
        def _():
            for k in range(1, N_HEAD):
                origin = lax.rem(me + N_HEAD - k, N_HEAD)
                landed = heads.at[it, :, 0, pl.ds(pl.multiple_of(origin * ROWS, 16), ROWS)]
                pltpu.make_async_copy(landed, landed, a2a_recv.at[it, k - 1]).wait()
            own_piece(it).wait()
            send_stage(it, 1)

        @pl.when((it >= 1) & (it < GROUP + 1))
        def _():
            wait_stage(it - 1, 2)
            send_stage(it - 1, 2)

        @pl.when((it >= 2) & (it < GROUP + 2))
        def _():
            wait_stage(it - 2, 3)
            send_stage(it - 2, 3)

        @pl.when(it >= 3)
        def _():
            wait_stage(it - 3, 4)
            attend(it - 3)

        return carry

    lax.fori_loop(0, GROUP + 3, step, 0)

    fetch_weight.wait()

    def project(c, carry):
        columns = pl.ds(pl.multiple_of(c * 512, 512), 512)
        out_ref[:, columns] = jnp.dot(
            attended[...], weight[:, columns], preferred_element_type=jnp.float32
        ).astype(jnp.bfloat16)
        return carry

    lax.fori_loop(0, D // 512, project, 0)

    def finish(j, carry):
        for k in range(1, N_HEAD):
            to_peer(j, k).wait_send()
        for index, route in enumerate(routes):
            @pl.when(route[4])
            def _():
                route_copy(j, index).wait_send()
        return carry

    lax.fori_loop(0, GROUP, finish, 0)


def attention(qkv, band, out_weight):
    return pl.pallas_call(
        attention_kernel,
        out_shape=jax.ShapeDtypeStruct((BLOCK, D), jnp.bfloat16),
        in_specs=[
            pl.BlockSpec(memory_space=pl.ANY),
            pl.BlockSpec(memory_space=pltpu.SMEM),
            pl.BlockSpec(memory_space=pl.ANY),
        ],
        out_specs=pl.BlockSpec(memory_space=pltpu.VMEM),
        scratch_shapes=[
            pltpu.VMEM((GROUP, 3, SLOTS, BLOCK, HD), jnp.bfloat16),
            pltpu.VMEM((BLOCK, INNER), jnp.bfloat16),
            pltpu.VMEM((INNER, D), jnp.bfloat16),
            pltpu.SemaphoreType.DMA((GROUP, N_HEAD - 1)),
            pltpu.SemaphoreType.DMA((GROUP, N_HEAD - 1)),
            pltpu.SemaphoreType.DMA((GROUP,)),
            pltpu.SemaphoreType.DMA((GROUP, 14)),
            pltpu.SemaphoreType.DMA((GROUP, SLOTS - 1)),
            pltpu.SemaphoreType.DMA,
        ],
        compiler_params=pltpu.CompilerParams(
            collective_id=0, has_side_effects=True, vmem_limit_bytes=56 * MIB
        ),
        name="attention",
    )(qkv, band, out_weight)


def rounded(values):
    narrow = lax.optimization_barrier(values.astype(jnp.bfloat16))
    return narrow.astype(jnp.float32)


def modulate(residual_state, shift_row, scale_row):
    average = jnp.mean(residual_state, axis=-1, keepdims=True)
    centered = residual_state - average
    variance = jnp.mean(centered * centered, axis=-1, keepdims=True)
    normal_form = centered * lax.rsqrt(variance + 1e-06)
    return (normal_form * (1.0 + scale_row) + shift_row).astype(jnp.bfloat16)


def shards(resid, qkv, band, out_weight, modulation, up_weight, down_weight):
    head_count = lax.axis_size("head")
    head_index = lax.axis_index("head")
    partial_value = attention(jnp.transpose(qkv, (1, 0, 2)), band, out_weight)
    rows_dev = BLOCK // head_count
    first_row = head_index * rows_dev
    branch = lax.psum(partial_value, "head").astype(jnp.float32)
    residual_state = resid.astype(jnp.float32) + modulation[0] * branch
    normed = modulate(residual_state, modulation[1], modulation[2])
    state_rows = lax.dynamic_slice_in_dim(residual_state, first_row, rows_dev, 0)
    projected = jnp.dot(
        normed,
        lax.all_gather(up_weight, "frame", axis=0, tiled=True),
        preferred_element_type=jnp.float32,
    )
    hidden = jax.nn.gelu(projected, approximate=True).astype(jnp.bfloat16)
    down_terms = rounded(
        jnp.dot(
            hidden,
            lax.all_gather(down_weight, "frame", axis=1, tiled=True),
            preferred_element_type=jnp.float32,
        )
    )
    ffn_out = lax.psum_scatter(
        down_terms.astype(jnp.bfloat16), "head", scatter_dimension=0, tiled=True
    ).astype(jnp.float32)
    return (state_rows + modulation[3] * ffn_out).astype(jnp.bfloat16)


def solution(mesh):
    in_specs = (
        P("frame", None),
        P(("frame", "head"), None, None),
        P("frame", None),
        P("head", None),
        P(),
        P("frame", "head"),
        P("head", "frame"),
    )
    out_specs = P(("frame", "head"), None)
    return jax.shard_map(shards, mesh=mesh, in_specs=in_specs, out_specs=out_specs, check_vma=False)
```

```python
import functools
import math

import jax
import jax.numpy as jnp
from jax import lax
from jax.experimental import pallas as pl
from jax.experimental.pallas import tpu as pltpu
from jax.sharding import PartitionSpec as P

HD = 128
SLOTS = 9
BLOCK = 384
NBLK = 32
N_HEAD = 8
ROWS = BLOCK // N_HEAD
GROUP = 5
INNER = GROUP * HD
D = 5120
MESH = pl.DeviceIdType.MESH
MIB = 2**20

partner_offsets = (0, -8, -4, -2, -1, 1, 2, 4, 8)
SLOT = {offset: slot for slot, offset in enumerate(partner_offsets)}
QUERY_ROWS = 128
SCALE_LOG2 = math.log2(math.e) / math.sqrt(HD)


def attention_kernel(
    qkv_ref, band_ref, weight_ref, out_ref,
    heads, attended, weight,
    a2a_send, a2a_recv, own_sem, halo_send, halo_recv, weight_sem,
):
    me = lax.axis_index("head")
    block = lax.axis_index("frame")
    x = lax.rem(block, 4)
    row_start = block - x

    def frame_device(frame):
        return {"head": me, "frame": frame}

    def head_device(head):
        return {"head": head, "frame": block}

    barrier = pltpu.get_barrier_semaphore()
    for k in range(1, N_HEAD):
        pl.semaphore_signal(barrier, inc=1, device_id=head_device(lax.rem(me + k, N_HEAD)), device_id_type=MESH)
    for k in range(1, 4):
        pl.semaphore_signal(barrier, inc=1, device_id=frame_device(row_start + lax.rem(x + k, 4)), device_id_type=MESH)
    for k in (4, NBLK - 4):
        pl.semaphore_signal(barrier, inc=1, device_id=frame_device(lax.rem(block + k, NBLK)), device_id_type=MESH)
    pl.semaphore_wait(barrier, N_HEAD - 1 + 3 + 2)

    fetch_weight = pltpu.make_async_copy(weight_ref, weight, weight_sem)
    my_rows = pl.ds(pl.multiple_of(me * ROWS, 16), ROWS)

    def to_peer(j, k):
        peer = lax.rem(me + k, N_HEAD)
        columns = pl.ds(pl.multiple_of(peer * INNER + j * HD, HD), HD)
        return pltpu.make_async_remote_copy(
            qkv_ref.at[:, :, columns], heads.at[j, :, 0, my_rows],
            a2a_send.at[j, k - 1], a2a_recv.at[j, k - 1],
            device_id=head_device(peer), device_id_type=MESH,
        )

    def own_piece(j):
        columns = pl.ds(pl.multiple_of(me * INNER + j * HD, HD), HD)
        return pltpu.make_async_copy(
            qkv_ref.at[:, :, columns], heads.at[j, :, 0, my_rows], own_sem.at[j]
        )

    def send_heads(j, carry):
        for k in (4, 3, 5, 2, 6, 1, 7):
            to_peer(j, k).start()
        own_piece(j).start()
        return carry

    lax.fori_loop(0, GROUP, send_heads, 0)
    fetch_weight.start()

    low4, high4 = block >= 4, block < NBLK - 4
    routes = (
        (1, 0, -4, block + 4, high4),
        (1, 0, 4, block - 4, low4),
        (1, 0, -1, block + 1, x < 3),
        (1, 0, 1, block - 1, x > 0),
        (2, -4, -8, block + 4, low4 & high4),
        (2, 4, 8, block - 4, low4 & high4),
        (2, -4, -1, row_start, (x == 3) & low4),
        (2, 4, 1, row_start + 3, (x == 0) & high4),
        (2, -1, -2, block + 1, (x == 1) | (x == 2)),
        (2, 1, 2, block - 1, (x == 1) | (x == 2)),
        (2, -4, -2, row_start, (x == 2) & low4),
        (2, 4, 2, row_start + 3, (x == 1) & high4),
        (3, -1, -2, block + 1, (x == 0) & low4),
        (3, 1, 2, block - 1, (x == 3) & high4),
    )
    arrivals = (
        (2, -4, low4),
        (2, 4, high4),
        (2, -1, x > 0),
        (2, 1, x < 3),
        (3, -1, (x == 0) & low4),
        (3, 1, (x == 3) & high4),
        (4, -2, block >= 2),
        (4, 2, block < NBLK - 2),
        (4, -8, block >= 8),
        (4, 8, block < NBLK - 8),
    )

    def route_copy(j, index):
        _, source, target, frame, _ = routes[index]
        return pltpu.make_async_remote_copy(
            heads.at[j, 1:3, SLOT[source]], heads.at[j, 1:3, SLOT[target]],
            halo_send.at[j, index], halo_recv.at[j, SLOT[target] - 1],
            device_id=frame_device(jnp.clip(frame, 0, NBLK - 1)), device_id_type=MESH,
        )

    def send_stage(j, stage):
        for index, route in enumerate(routes):
            if route[0] == stage:
                @pl.when(route[4])
                def _():
                    route_copy(j, index).start()

    def wait_stage(j, stage):
        for before, slot, when in arrivals:
            if before == stage:
                @pl.when(when)
                def _():
                    landed = heads.at[j, 1:3, SLOT[slot]]
                    pltpu.make_async_copy(landed, landed, halo_recv.at[j, SLOT[slot] - 1]).wait()

    for offset in partner_offsets[1:]:
        partner = block + offset

        @pl.when((partner < 0) | (partner >= NBLK))
        def _():
            heads[:, 1:3, SLOT[offset]] = jnp.zeros((GROUP, 2, BLOCK, HD), jnp.bfloat16)

    def attend(j):
        widths = []
        for slot, offset in enumerate(partner_offsets):
            partner = block + offset
            present = (partner >= 0) & (partner < NBLK)
            widths.append(jnp.where(present, band_ref[0, slot], 0))
        keys = heads[j, 1].reshape(SLOTS * BLOCK, HD)
        values = heads[j, 2].reshape(SLOTS * BLOCK, HD)
        columns = pl.ds(pl.multiple_of(j * HD, HD), HD)
        for first in range(0, BLOCK, QUERY_ROWS):
            queries = heads[j, 0, 0, first:first + QUERY_ROWS]
            scores = lax.dot_general(
                queries, keys, (((1,), (1,)), ((), ())), preferred_element_type=jnp.float32
            )
            row = lax.broadcasted_iota(jnp.int32, (QUERY_ROWS, BLOCK), 0) + first
            column = lax.broadcasted_iota(jnp.int32, (QUERY_ROWS, BLOCK), 1)
            distance = jnp.abs(row - column)
            parts = []
            for slot in range(SLOTS):
                part = scores[:, slot * BLOCK:(slot + 1) * BLOCK]
                parts.append(jnp.where(distance < widths[slot], part, -1e30))
            top = functools.reduce(jnp.maximum, parts)
            row_max = jnp.max(top, axis=1, keepdims=True)
            weights = [jnp.exp2((part - row_max) * SCALE_LOG2) for part in parts]
            denominator = jnp.sum(functools.reduce(jnp.add, weights), axis=1, keepdims=True)
            probabilities = jnp.concatenate([w.astype(jnp.bfloat16) for w in weights], axis=1)
            summed = jnp.dot(probabilities, values, preferred_element_type=jnp.float32)
            attended[first:first + QUERY_ROWS, columns] = (summed / denominator).astype(jnp.bfloat16)

    def step(it, carry):
        @pl.when(it < GROUP)
        def _():
            for k in range(1, N_HEAD):
                origin = lax.rem(me + N_HEAD - k, N_HEAD)
                landed = heads.at[it, :, 0, pl.ds(pl.multiple_of(origin * ROWS, 16), ROWS)]
                pltpu.make_async_copy(landed, landed, a2a_recv.at[it, k - 1]).wait()
            own_piece(it).wait()
            send_stage(it, 1)

        @pl.when((it >= 1) & (it < GROUP + 1))
        def _():
            wait_stage(it - 1, 2)
            send_stage(it - 1, 2)

        @pl.when((it >= 2) & (it < GROUP + 2))
        def _():
            wait_stage(it - 2, 3)
            send_stage(it - 2, 3)

        @pl.when(it >= 3)
        def _():
            wait_stage(it - 3, 4)
            attend(it - 3)

        return carry

    lax.fori_loop(0, GROUP + 3, step, 0)

    fetch_weight.wait()

    def project(c, carry):
        columns = pl.ds(pl.multiple_of(c * 512, 512), 512)
        out_ref[:, columns] = jnp.dot(
            attended[...], weight[:, columns], preferred_element_type=jnp.float32
        ).astype(jnp.bfloat16)
        return carry

    lax.fori_loop(0, D // 512, project, 0)

    def finish(j, carry):
        for k in range(1, N_HEAD):
            to_peer(j, k).wait_send()
        for index, route in enumerate(routes):
            @pl.when(route[4])
            def _():
                route_copy(j, index).wait_send()
        return carry

    lax.fori_loop(0, GROUP, finish, 0)


def attention(qkv, band, out_weight):
    return pl.pallas_call(
        attention_kernel,
        out_shape=jax.ShapeDtypeStruct((BLOCK, D), jnp.bfloat16),
        in_specs=[
            pl.BlockSpec(memory_space=pl.ANY),
            pl.BlockSpec(memory_space=pltpu.SMEM),
            pl.BlockSpec(memory_space=pl.ANY),
        ],
        out_specs=pl.BlockSpec(memory_space=pltpu.VMEM),
        scratch_shapes=[
            pltpu.VMEM((GROUP, 3, SLOTS, BLOCK, HD), jnp.bfloat16),
            pltpu.VMEM((BLOCK, INNER), jnp.bfloat16),
            pltpu.VMEM((INNER, D), jnp.bfloat16),
            pltpu.SemaphoreType.DMA((GROUP, N_HEAD - 1)),
            pltpu.SemaphoreType.DMA((GROUP, N_HEAD - 1)),
            pltpu.SemaphoreType.DMA((GROUP,)),
            pltpu.SemaphoreType.DMA((GROUP, 14)),
            pltpu.SemaphoreType.DMA((GROUP, SLOTS - 1)),
            pltpu.SemaphoreType.DMA,
        ],
        compiler_params=pltpu.CompilerParams(
            collective_id=0, has_side_effects=True, vmem_limit_bytes=56 * MIB
        ),
        name="attention",
    )(qkv, band, out_weight)


HALF = D // 2
UNITS = 432
MAIN = 384
TAIL = UNITS - MAIN
PACK = 896
WROWS = 160


def feed_forward_kernel(
    partial_ref, resid_ref, modulation_ref, pack_own_ref, pack_other_ref, out_ref,
    weights, sib1, opposite, pairs, state, resid_rows, normed, hidden, down, sib2, ring,
    local_sem, w_send, w_recv, s1_send, s1_recv, r1_send, r1_recv,
    ag_send, ag_recv, agsib_send, agsib_recv, s2_send, s2_recv, r2_send, r2_recv,
):
    me = lax.axis_index("head")
    frame = lax.axis_index("frame")
    z_hi, core = me // 2, lax.rem(me, 2)
    z_lo, yx = frame // 16, lax.rem(frame, 16)
    y, x = yx // 4, lax.rem(yx, 4)
    z = z_hi * 2 + z_lo
    halves = (pl.ds(0, HALF), pl.ds(HALF, HALF))

    def z_device(other):
        return {"head": (other // 2) * 2 + core, "frame": lax.rem(other, 2) * 16 + yx}

    sibling = {"head": z_hi * 2 + 1 - core, "frame": frame}
    above, below = z_device(lax.rem(z + 1, 8)), z_device(lax.rem(z + 7, 8))
    above2, below2 = z_device(lax.rem(z + 2, 8)), z_device(lax.rem(z + 6, 8))
    x_peers = [{"head": me, "frame": z_lo * 16 + y * 4 + lax.rem(x + k, 4)} for k in (1, 2, 3)]
    y_peers = [{"head": me, "frame": z_lo * 16 + lax.rem(y + k, 4) * 4 + x} for k in (1, 2, 3)]
    other_plane = z_device(z + 1 - 2 * z_lo)

    barrier = pltpu.get_barrier_semaphore()
    greeted = [sibling, above, below, above2, below2] + x_peers + y_peers
    for device in greeted:
        pl.semaphore_signal(barrier, inc=1, device_id=device, device_id_type=MESH)
    pl.semaphore_wait(barrier, len(greeted))

    def remote(source, target, send, recv, device):
        return pltpu.make_async_remote_copy(
            source, target, send, recv, device_id=device, device_id_type=MESH
        )

    started = []

    def go(copy):
        copy.start()
        started.append(copy)

    my_rows = pl.ds(pl.multiple_of(me * ROWS, 16), ROWS)
    fetch_resid = pltpu.make_async_copy(resid_ref.at[my_rows], resid_rows, local_sem.at[0])
    fetch_resid.start()
    fetch_pack = pltpu.make_async_copy(pack_own_ref, weights.at[z_lo, y, x], local_sem.at[1])
    fetch_pack.start()

    order = [lax.rem(z_hi + k, 4) for k in (2, 1, 3, 0)]
    s1 = [
        remote(partial_ref.at[q, 1 - core], sib1.at[q], s1_send.at[i], s1_recv.at[i], sibling)
        for i, q in enumerate(order)
    ]
    for copy in s1:
        go(copy)

    cross = remote(pack_other_ref, weights.at[z_lo, y, x], w_send.at[0], w_recv.at[0], other_plane)
    go(cross)
    first_a = [
        remote(pack_own_ref, weights.at[z_lo, y, x], w_send.at[1 + i], w_recv.at[1 + i], device)
        for i, device in enumerate(x_peers)
    ]
    for copy in first_a:
        go(copy)

    def pair(q, columns):
        return (
            partial_ref[q, core, :, columns].astype(jnp.float32)
            + sib1[q, :, columns].astype(jnp.float32)
        )

    s1[0].wait_recv()
    q = order[0]
    for half in (0, 1):
        sib1[q, :, halves[half]] = pair(q, halves[half]).astype(jnp.bfloat16)
        go(remote(
            sib1.at[q, :, halves[half]], opposite.at[half],
            r1_send.at[half], r1_recv.at[half], (above2, below2)[half],
        ))
    opposites = started[-2:]
    finals = [None] * 4
    for way in (0, 1):
        s1[1 + way].wait_recv()
        q, half = order[1 + way], 1 - way
        sib1[q, :, halves[half]] = pair(q, halves[half]).astype(jnp.bfloat16)
        index = 2 + way * 2 + half
        go(remote(
            sib1.at[q, :, halves[half]], pairs.at[way, :, halves[half]],
            r1_send.at[index], r1_recv.at[index], (above2, below2)[way],
        ))
        finals[way * 2 + half] = started[-1]

    cross.wait_recv()
    first_b = [
        remote(
            weights.at[1 - z_lo, y, x], weights.at[1 - z_lo, y, x],
            w_send.at[4 + i], w_recv.at[4 + i], device,
        )
        for i, device in enumerate(y_peers)
    ]
    for copy in first_b:
        go(copy)

    for way in (0, 1):
        q, half = order[1 + way], way
        opposites[half].wait_recv()
        total = pair(q, halves[half]) + opposite[half].astype(jnp.float32)
        sib1[q, :, halves[half]] = total.astype(jnp.bfloat16)
        index = 2 + way * 2 + half
        go(remote(
            sib1.at[q, :, halves[half]], pairs.at[way, :, halves[half]],
            r1_send.at[index], r1_recv.at[index], (above2, below2)[way],
        ))
        finals[way * 2 + half] = started[-1]

    fetch_pack.wait()
    for copy in first_a:
        copy.wait_recv()
    second_a = [
        remote(
            weights.at[z_lo, y], weights.at[z_lo, y], w_send.at[7 + i], w_recv.at[7 + i], device
        )
        for i, device in enumerate(y_peers)
    ]
    for copy in second_a:
        go(copy)
    for copy in first_b:
        copy.wait_recv()
    second_b = [
        remote(
            weights.at[1 - z_lo, :, x], weights.at[1 - z_lo, :, x],
            w_send.at[10 + i], w_recv.at[10 + i], device,
        )
        for i, device in enumerate(x_peers)
    ]
    for copy in second_b:
        go(copy)

    fetch_resid.wait()
    s1[3].wait_recv()
    for copy in finals:
        copy.wait_recv()
    for half in (0, 1):
        columns = halves[half]
        branch = (
            pair(z_hi, columns)
            + pairs[0, :, columns].astype(jnp.float32)
            + pairs[1, :, columns].astype(jnp.float32)
        )
        state[:, columns] = (
            resid_rows[:, columns].astype(jnp.float32) + modulation_ref[0:1, columns] * branch
        )
    for first in range(0, ROWS, 16):
        rows = slice(first, first + 16)
        value = state[rows]
        average = jnp.mean(value, axis=-1, keepdims=True)
        centered = value - average
        variance = jnp.mean(centered * centered, axis=-1, keepdims=True)
        normal_form = centered * lax.rsqrt(variance + 1e-06)
        normed[z, core, rows] = (
            normal_form * (1.0 + modulation_ref[2:3]) + modulation_ref[1:2]
        ).astype(jnp.bfloat16)

    def shard(distance):
        return lax.rem(z + distance + 8, 8)

    gathered = []

    def to_sibling(view, index):
        copy = remote(view, view, agsib_send.at[index], agsib_recv.at[index], sibling)
        go(copy)
        gathered.append(copy)

    hops = {}

    def hop(way, step):
        origin = shard((1 - step) * (1 - 2 * way))
        view = normed.at[origin, core]
        if step == 4:
            view = view.at[:, halves[way]]
        hops[way, step] = remote(
            view, view, ag_send.at[way, step - 1], ag_recv.at[way, step - 1], (above, below)[way]
        )
        go(hops[way, step])

    hop(0, 1)
    hop(1, 1)
    to_sibling(normed.at[z, core], 0)
    for step in (1, 2, 3, 4):
        for way in (0, 1):
            hops[way, step].wait_recv()
            view = normed.at[shard(-step * (1 - 2 * way)), core]
            if step < 4:
                hop(way, step + 1)
            else:
                view = view.at[:, halves[way]]
            to_sibling(view, 1 + (step - 1) * 2 + way)
    for copy in gathered:
        copy.wait_recv()
    for copy in second_a + second_b:
        copy.wait_recv()

    def up(i, carry):
        rows = normed[pl.ds(4 * i, 4)].reshape(4 * 2 * ROWS, D)
        total = None
        for c in range(4):
            weight = weights[c // 2, 2 * (c % 2):2 * (c % 2) + 2, :, :, 0:512].reshape(8 * WROWS, 512)
            product = jnp.dot(
                rows[:, c * 1280:(c + 1) * 1280], weight, preferred_element_type=jnp.float32
            )
            total = product if total is None else total + product
        active = jax.nn.gelu(total, approximate=True)
        lane = lax.broadcasted_iota(jnp.int32, (8 * ROWS, 128), 1)
        tail = pltpu.roll(active[:, MAIN:512], TAIL, 1)
        tail = jnp.where((lane >= TAIL) & (lane < 2 * TAIL), tail, 0.0)
        target = pl.ds(pl.multiple_of(i * 8 * ROWS, 16), 8 * ROWS)
        hidden[target, 0:128] = tail.astype(jnp.bfloat16)
        hidden[target, 128:512] = active[:, 0:MAIN].astype(jnp.bfloat16)
        return carry

    lax.fori_loop(0, 2, up, 0)

    def project(c, carry):
        weight = weights[c // 4, lax.rem(c, 4), :, :, MAIN:PACK].reshape(4 * WROWS, 512)
        columns = pl.ds(pl.multiple_of(c * 4 * WROWS, 128), 4 * WROWS)
        product = lax.dot_general(
            hidden[...], weight, (((1,), (1,)), ((), ())), preferred_element_type=jnp.float32
        )
        down[:, :, :, columns] = product.astype(jnp.bfloat16).reshape(8, 2, ROWS, 4 * WROWS)
        return carry

    s2 = {}
    distances = (4, 3, -3, 2, -2, 1, -1, 0)
    for half in (0, 1):
        lax.fori_loop(4 * half, 4 * half + 4, project, 0)
        for i, distance in enumerate(distances):
            q = shard(distance)
            s2[distance, half] = remote(
                down.at[q, 1 - core, :, halves[half]], sib2.at[q, :, halves[half]],
                s2_send.at[half, i], s2_recv.at[half, i], sibling,
            )
            go(s2[distance, half])

    def pair2(q, columns):
        return (
            down[q, core, :, columns].astype(jnp.float32)
            + sib2[q, :, columns].astype(jnp.float32)
        )

    sums = {}

    def ring_step(way, half, step):
        distance = (5 - step) * (1 - 2 * way)
        key = 4 if step == 1 else distance
        q, columns = shard(distance), halves[half]
        s2[key, half].wait_recv()
        total = pair2(q, columns)
        if (way, half, step - 1) in sums:
            sums[way, half, step - 1].wait_recv()
            total = total + ring[way, half, step - 2].astype(jnp.float32)
        sib2[q, :, columns] = total.astype(jnp.bfloat16)
        sums[way, half, step] = remote(
            sib2.at[q, :, columns], ring.at[way, half, step - 1],
            r2_send.at[way, half, step - 1], r2_recv.at[way, half, step - 1],
            (above, below)[way],
        )
        go(sums[way, half, step])

    ring_step(0, 0, 1)
    ring_step(1, 1, 1)
    for step in (2, 3, 4):
        ring_step(0, 1, step)
        ring_step(1, 0, step)
        ring_step(0, 0, step)
        ring_step(1, 1, step)
    for half in (1, 0):
        columns = halves[half]
        s2[0, half].wait_recv()
        ffn = pair2(z, columns)
        for way in ((0, 1) if half else (1, 0)):
            sums[way, half, 4].wait_recv()
            ffn = ffn + ring[way, half, 3].astype(jnp.float32)
        out_ref[:, columns] = (
            state[:, columns] + modulation_ref[3:4, columns] * ffn
        ).astype(jnp.bfloat16)

    for copy in started:
        copy.wait_send()


def feed_forward(partial_value, resid, modulation, pack_own, pack_other):
    dma = pltpu.SemaphoreType.DMA
    bf16 = jnp.bfloat16
    return pl.pallas_call(
        feed_forward_kernel,
        out_shape=jax.ShapeDtypeStruct((ROWS, D), bf16),
        in_specs=[
            pl.BlockSpec(memory_space=pltpu.VMEM),
            pl.BlockSpec(memory_space=pl.ANY),
            pl.BlockSpec(memory_space=pltpu.VMEM),
            pl.BlockSpec(memory_space=pl.ANY),
            pl.BlockSpec(memory_space=pl.ANY),
        ],
        out_specs=pl.BlockSpec(memory_space=pltpu.VMEM),
        scratch_shapes=[
            pltpu.VMEM((2, 4, 4, WROWS, PACK), bf16),
            pltpu.VMEM((4, ROWS, D), bf16),
            pltpu.VMEM((2, ROWS, HALF), bf16),
            pltpu.VMEM((2, ROWS, D), bf16),
            pltpu.VMEM((ROWS, D), jnp.float32),
            pltpu.VMEM((ROWS, D), bf16),
            pltpu.VMEM((8, 2, ROWS, D), bf16),
            pltpu.VMEM((16 * ROWS, 512), bf16),
            pltpu.VMEM((8, 2, ROWS, D), bf16),
            pltpu.VMEM((8, ROWS, D), bf16),
            pltpu.VMEM((2, 2, 4, ROWS, HALF), bf16),
            dma((2,)), dma((13,)), dma((13,)), dma((4,)), dma((4,)), dma((6,)), dma((6,)),
            dma((2, 4)), dma((2, 4)), dma((9,)), dma((9,)),
            dma((2, 8)), dma((2, 8)), dma((2, 2, 4)), dma((2, 2, 4)),
        ],
        compiler_params=pltpu.CompilerParams(
            collective_id=1, has_side_effects=True, vmem_limit_bytes=58 * MIB
        ),
        name="feed_forward",
    )(partial_value, resid, modulation, pack_own, pack_other)


def pack_weights(up_weight, down_rows, first):
    cut = first + MAIN
    return jnp.concatenate(
        [
            up_weight[:, first:cut],
            up_weight[:, cut:first + UNITS],
            down_rows[:, cut:first + UNITS],
            jnp.zeros((WROWS, PACK - MAIN - 2 * TAIL - MAIN), jnp.bfloat16),
            down_rows[:, first:cut],
        ],
        axis=1,
    )


def shards(resid, qkv, band, out_weight, modulation, up_weight, down_weight):
    z_lo = lax.axis_index("frame") // 16
    down_rows = jnp.transpose(down_weight)
    packs = [pack_weights(up_weight, down_rows, first) for first in (0, UNITS)]
    pack_own = jnp.where(z_lo == 0, packs[0], packs[1])
    pack_other = jnp.where(z_lo == 0, packs[1], packs[0])
    partial_value = attention(jnp.transpose(qkv, (1, 0, 2)), band, out_weight)
    return feed_forward(
        partial_value.reshape(4, 2, ROWS, D), resid, modulation, pack_own, pack_other
    )


def solution(mesh):
    in_specs = (
        P("frame", None),
        P(("frame", "head"), None, None),
        P("frame", None),
        P("head", None),
        P(),
        P("frame", "head"),
        P("head", "frame"),
    )
    out_specs = P(("frame", "head"), None)
    return jax.shard_map(shards, mesh=mesh, in_specs=in_specs, out_specs=out_specs, check_vma=False)
```

```python
import functools
import math

import jax
import jax.numpy as jnp
from jax import lax
from jax.experimental import pallas as pl
from jax.experimental.pallas import tpu as pltpu
from jax.sharding import PartitionSpec as P

HD = 128
SLOTS = 9
BLOCK = 384
NBLK = 32
N_HEAD = 8
ROWS = BLOCK // N_HEAD
GROUP = 5
INNER = GROUP * HD
D = 5120
MESH = pl.DeviceIdType.MESH
MIB = 2**20

partner_offsets = (0, -8, -4, -2, -1, 1, 2, 4, 8)
SLOT = {offset: slot for slot, offset in enumerate(partner_offsets)}
QUERY_ROWS = 128
SCALE_LOG2 = math.log2(math.e) / math.sqrt(HD)


def attention_kernel(
    qkv_ref, band_ref, weight_ref, out_ref,
    heads, attended, weight,
    a2a_send, a2a_recv, own_sem, halo_send, halo_recv, weight_sem,
):
    me = lax.axis_index("head")
    block = lax.axis_index("frame")
    x = lax.rem(block, 4)
    row_start = block - x

    def frame_device(frame):
        return {"head": me, "frame": frame}

    def head_device(head):
        return {"head": head, "frame": block}

    barrier = pltpu.get_barrier_semaphore()
    for k in range(1, N_HEAD):
        pl.semaphore_signal(barrier, inc=1, device_id=head_device(lax.rem(me + k, N_HEAD)), device_id_type=MESH)
    for k in range(1, 4):
        pl.semaphore_signal(barrier, inc=1, device_id=frame_device(row_start + lax.rem(x + k, 4)), device_id_type=MESH)
    for k in (4, NBLK - 4):
        pl.semaphore_signal(barrier, inc=1, device_id=frame_device(lax.rem(block + k, NBLK)), device_id_type=MESH)
    pl.semaphore_wait(barrier, N_HEAD - 1 + 3 + 2)

    fetch_weight = pltpu.make_async_copy(weight_ref, weight, weight_sem)
    my_rows = pl.ds(pl.multiple_of(me * ROWS, 16), ROWS)

    def to_peer(j, k):
        peer = lax.rem(me + k, N_HEAD)
        columns = pl.ds(pl.multiple_of(peer * INNER + j * HD, HD), HD)
        return pltpu.make_async_remote_copy(
            qkv_ref.at[:, :, columns], heads.at[j, :, 0, my_rows],
            a2a_send.at[j, k - 1], a2a_recv.at[j, k - 1],
            device_id=head_device(peer), device_id_type=MESH,
        )

    def own_piece(j):
        columns = pl.ds(pl.multiple_of(me * INNER + j * HD, HD), HD)
        return pltpu.make_async_copy(
            qkv_ref.at[:, :, columns], heads.at[j, :, 0, my_rows], own_sem.at[j]
        )

    def send_heads(j, carry):
        for k in (4, 3, 5, 2, 6, 1, 7):
            to_peer(j, k).start()
        own_piece(j).start()
        return carry

    lax.fori_loop(0, 2, send_heads, 0)
    fetch_weight.start()

    low4, high4 = block >= 4, block < NBLK - 4
    routes = (
        (1, 0, -4, block + 4, high4),
        (1, 0, 4, block - 4, low4),
        (1, 0, -1, block + 1, x < 3),
        (1, 0, 1, block - 1, x > 0),
        (2, -4, -8, block + 4, low4 & high4),
        (2, 4, 8, block - 4, low4 & high4),
        (2, -4, -1, row_start, (x == 3) & low4),
        (2, 4, 1, row_start + 3, (x == 0) & high4),
        (2, -1, -2, block + 1, (x == 1) | (x == 2)),
        (2, 1, 2, block - 1, (x == 1) | (x == 2)),
        (2, -4, -2, row_start, (x == 2) & low4),
        (2, 4, 2, row_start + 3, (x == 1) & high4),
        (3, -1, -2, block + 1, (x == 0) & low4),
        (3, 1, 2, block - 1, (x == 3) & high4),
    )
    arrivals = (
        (2, -4, low4),
        (2, 4, high4),
        (2, -1, x > 0),
        (2, 1, x < 3),
        (3, -1, (x == 0) & low4),
        (3, 1, (x == 3) & high4),
        (4, -2, block >= 2),
        (4, 2, block < NBLK - 2),
        (4, -8, block >= 8),
        (4, 8, block < NBLK - 8),
    )

    def route_copy(j, index):
        _, source, target, frame, _ = routes[index]
        return pltpu.make_async_remote_copy(
            heads.at[j, 1:3, SLOT[source]], heads.at[j, 1:3, SLOT[target]],
            halo_send.at[j, index], halo_recv.at[j, SLOT[target] - 1],
            device_id=frame_device(jnp.clip(frame, 0, NBLK - 1)), device_id_type=MESH,
        )

    def send_stage(j, stage):
        for index, route in enumerate(routes):
            if route[0] == stage:
                @pl.when(route[4])
                def _():
                    route_copy(j, index).start()

    def wait_stage(j, stage):
        for before, slot, when in arrivals:
            if before == stage:
                @pl.when(when)
                def _():
                    landed = heads.at[j, 1:3, SLOT[slot]]
                    pltpu.make_async_copy(landed, landed, halo_recv.at[j, SLOT[slot] - 1]).wait()

    for offset in partner_offsets[1:]:
        partner = block + offset

        @pl.when((partner < 0) | (partner >= NBLK))
        def _():
            heads[:, 1:3, SLOT[offset]] = jnp.zeros((GROUP, 2, BLOCK, HD), jnp.bfloat16)

    def attend(j):
        widths = []
        for slot, offset in enumerate(partner_offsets):
            partner = block + offset
            present = (partner >= 0) & (partner < NBLK)
            widths.append(jnp.where(present, band_ref[0, slot], 0))
        keys = heads[j, 1].reshape(SLOTS * BLOCK, HD)
        values = heads[j, 2].reshape(SLOTS * BLOCK, HD)
        columns = pl.ds(pl.multiple_of(j * HD, HD), HD)
        for first in range(0, BLOCK, QUERY_ROWS):
            queries = heads[j, 0, 0, first:first + QUERY_ROWS]
            scores = lax.dot_general(
                queries, keys, (((1,), (1,)), ((), ())), preferred_element_type=jnp.float32
            )
            row = lax.broadcasted_iota(jnp.int32, (QUERY_ROWS, BLOCK), 0) + first
            column = lax.broadcasted_iota(jnp.int32, (QUERY_ROWS, BLOCK), 1)
            distance = jnp.abs(row - column)
            parts = []
            for slot in range(SLOTS):
                part = scores[:, slot * BLOCK:(slot + 1) * BLOCK]
                parts.append(jnp.where(distance < widths[slot], part, -1e30))
            top = functools.reduce(jnp.maximum, parts)
            row_max = jnp.max(top, axis=1, keepdims=True)
            weights = [jnp.exp2((part - row_max) * SCALE_LOG2) for part in parts]
            denominator = jnp.sum(functools.reduce(jnp.add, weights), axis=1, keepdims=True)
            probabilities = jnp.concatenate([w.astype(jnp.bfloat16) for w in weights], axis=1)
            summed = jnp.dot(probabilities, values, preferred_element_type=jnp.float32)
            attended[first:first + QUERY_ROWS, columns] = (summed / denominator).astype(jnp.bfloat16)

    def step(it, carry):
        @pl.when(it < GROUP)
        def _():
            for k in range(1, N_HEAD):
                origin = lax.rem(me + N_HEAD - k, N_HEAD)
                landed = heads.at[it, :, 0, pl.ds(pl.multiple_of(origin * ROWS, 16), ROWS)]
                pltpu.make_async_copy(landed, landed, a2a_recv.at[it, k - 1]).wait()
            own_piece(it).wait()
            send_stage(it, 1)

        @pl.when(it < GROUP - 2)
        def _():
            send_heads(it + 2, 0)

        @pl.when((it >= 1) & (it < GROUP + 1))
        def _():
            wait_stage(it - 1, 2)
            send_stage(it - 1, 2)

        @pl.when((it >= 2) & (it < GROUP + 2))
        def _():
            wait_stage(it - 2, 3)
            send_stage(it - 2, 3)

        @pl.when(it >= 3)
        def _():
            wait_stage(it - 3, 4)
            attend(it - 3)

        return carry

    lax.fori_loop(0, GROUP + 3, step, 0)

    fetch_weight.wait()

    def project(c, carry):
        columns = pl.ds(pl.multiple_of(c * 512, 512), 512)
        out_ref[:, columns] = jnp.dot(
            attended[...], weight[:, columns], preferred_element_type=jnp.float32
        ).astype(jnp.bfloat16)
        return carry

    lax.fori_loop(0, D // 512, project, 0)

    def finish(j, carry):
        for k in range(1, N_HEAD):
            to_peer(j, k).wait_send()
        for index, route in enumerate(routes):
            @pl.when(route[4])
            def _():
                route_copy(j, index).wait_send()
        return carry

    lax.fori_loop(0, GROUP, finish, 0)


def attention(qkv, band, out_weight):
    return pl.pallas_call(
        attention_kernel,
        out_shape=jax.ShapeDtypeStruct((BLOCK, D), jnp.bfloat16),
        in_specs=[
            pl.BlockSpec(memory_space=pl.ANY),
            pl.BlockSpec(memory_space=pltpu.SMEM),
            pl.BlockSpec(memory_space=pl.ANY),
        ],
        out_specs=pl.BlockSpec(memory_space=pltpu.VMEM),
        scratch_shapes=[
            pltpu.VMEM((GROUP, 3, SLOTS, BLOCK, HD), jnp.bfloat16),
            pltpu.VMEM((BLOCK, INNER), jnp.bfloat16),
            pltpu.VMEM((INNER, D), jnp.bfloat16),
            pltpu.SemaphoreType.DMA((GROUP, N_HEAD - 1)),
            pltpu.SemaphoreType.DMA((GROUP, N_HEAD - 1)),
            pltpu.SemaphoreType.DMA((GROUP,)),
            pltpu.SemaphoreType.DMA((GROUP, 14)),
            pltpu.SemaphoreType.DMA((GROUP, SLOTS - 1)),
            pltpu.SemaphoreType.DMA,
        ],
        compiler_params=pltpu.CompilerParams(
            collective_id=0, has_side_effects=True, vmem_limit_bytes=56 * MIB
        ),
        name="attention",
    )(qkv, band, out_weight)


HALF = D // 2
UNITS = 432
MAIN = 384
TAIL = UNITS - MAIN
PACK = 896
WROWS = 160
STREAMS = 3
PART = ROWS // STREAMS
LAG = 1


def feed_forward_kernel(
    partial_ref, resid_ref, modulation_ref, up_ref, down_rows_ref, out_ref,
    weights, other_pack, sib1, opposite, pairs, state, resid_rows, normed, hidden, down, sib2, ring,
    local_sem, w_send, w_recv, s1_send, s1_recv, r1_send, r1_recv,
    ag_send, ag_recv, agsib_send, agsib_recv, s2_send, s2_recv, r2_send, r2_recv,
):
    me = lax.axis_index("head")
    frame = lax.axis_index("frame")
    z_hi, core = me // 2, lax.rem(me, 2)
    z_lo, yx = frame // 16, lax.rem(frame, 16)
    y, x = yx // 4, lax.rem(yx, 4)
    z = z_hi * 2 + z_lo
    halves = (pl.ds(0, HALF), pl.ds(HALF, HALF))

    def z_device(other):
        return {"head": (other // 2) * 2 + core, "frame": lax.rem(other, 2) * 16 + yx}

    sibling = {"head": z_hi * 2 + 1 - core, "frame": frame}
    above, below = z_device(lax.rem(z + 1, 8)), z_device(lax.rem(z + 7, 8))
    above2, below2 = z_device(lax.rem(z + 2, 8)), z_device(lax.rem(z + 6, 8))
    x_peers = [{"head": me, "frame": z_lo * 16 + y * 4 + lax.rem(x + k, 4)} for k in (1, 2, 3)]
    y_peers = [{"head": me, "frame": z_lo * 16 + lax.rem(y + k, 4) * 4 + x} for k in (1, 2, 3)]
    other_plane = z_device(z + 1 - 2 * z_lo)

    barrier = pltpu.get_barrier_semaphore()
    greeted = [sibling, above, below, above2, below2] + x_peers + y_peers
    for device in greeted:
        pl.semaphore_signal(barrier, inc=1, device_id=device, device_id_type=MESH)

    my_rows = pl.ds(pl.multiple_of(me * ROWS, 16), ROWS)
    fetch_resid = pltpu.make_async_copy(resid_ref.at[my_rows], resid_rows, local_sem.at[0])
    fetch_resid.start()

    lane = lax.broadcasted_iota(jnp.int32, (WROWS, 128), 1)
    blank = jnp.zeros((WROWS, 128 - 2 * TAIL), jnp.float32)
    tails = [
        jnp.concatenate([ref[:, 2 * MAIN:].astype(jnp.float32), blank], axis=1)
        for ref in (up_ref, down_rows_ref)
    ]
    up_tail = [tails[0], pltpu.roll(tails[0], 128 - TAIL, 1)]
    down_tail = [pltpu.roll(tails[1], TAIL, 1), tails[1]]
    mixed_tail = []
    for side in (0, 1):
        down_part = jnp.where(lane < 2 * TAIL, down_tail[side], 0.0)
        mixed_tail.append(jnp.where(lane < TAIL, up_tail[side], down_part))

    def pack(target, side):
        columns = pl.ds(pl.multiple_of(side * MAIN, 128), MAIN)
        target[:, 0:MAIN] = up_ref[:, columns]
        target[:, MAIN:512] = jnp.where(side == 0, mixed_tail[0], mixed_tail[1]).astype(jnp.bfloat16)
        target[:, 512:PACK] = down_rows_ref[:, columns]

    pack(other_pack, 1 - z_lo)
    pack(weights.at[z_lo, y, x], z_lo)

    pl.semaphore_wait(barrier, len(greeted))

    started = []

    def send(source, target, send_sem, recv_sem, device):
        copy = pltpu.make_async_remote_copy(
            source, target, send_sem, recv_sem, device_id=device, device_id_type=MESH
        )
        copy.start()
        started.append(copy)
        return copy

    order = [lax.rem(z_hi + k, 4) for k in (2, 1, 3, 0)]
    parts = [slice(r * PART, (r + 1) * PART) for r in range(STREAMS)]
    s1 = [
        [
            send(
                partial_ref.at[q, 1 - core, parts[r]], sib1.at[r, q],
                s1_send.at[r, i], s1_recv.at[r, i], sibling,
            )
            for i, q in enumerate(order)
        ]
        for r in range(STREAMS)
    ]

    cross = send(other_pack, weights.at[z_lo, y, x], w_send.at[0], w_recv.at[0], other_plane)
    first_a = [
        send(
            weights.at[z_lo, y, x], weights.at[z_lo, y, x],
            w_send.at[1 + i], w_recv.at[1 + i], device,
        )
        for i, device in enumerate(x_peers)
    ]
    first_b, second = [], []

    def weights_first():
        cross.wait_recv()
        view = weights.at[1 - z_lo, y, x]
        for i, device in enumerate(y_peers):
            first_b.append(send(view, view, w_send.at[4 + i], w_recv.at[4 + i], device))

    def weights_second():
        for copy in first_a:
            copy.wait_recv()
        view = weights.at[z_lo, y]
        for i, device in enumerate(y_peers):
            second.append(send(view, view, w_send.at[7 + i], w_recv.at[7 + i], device))
        for copy in first_b:
            copy.wait_recv()
        view = weights.at[1 - z_lo, :, x]
        for i, device in enumerate(x_peers):
            second.append(send(view, view, w_send.at[10 + i], w_recv.at[10 + i], device))

    def weights_here():
        for copy in second:
            copy.wait_recv()
        second.clear()

    def shard(distance):
        return lax.rem(z + distance + 8, 8)

    def up(r):
        rows = normed[r].reshape(16 * PART, D)
        total = None
        for c in range(4):
            weight = weights[c // 2, 2 * (c % 2):2 * (c % 2) + 2, :, :, 0:512].reshape(8 * WROWS, 512)
            product = jnp.dot(
                rows[:, c * 1280:(c + 1) * 1280], weight, preferred_element_type=jnp.float32
            )
            total = product if total is None else total + product
        active = jax.nn.gelu(total, approximate=True)
        place = lax.broadcasted_iota(jnp.int32, (16 * PART, 128), 1)
        tail = pltpu.roll(active[:, MAIN:512], TAIL, 1)
        tail = jnp.where((place >= TAIL) & (place < 2 * TAIL), tail, 0.0)
        hidden[:, 0:128] = tail.astype(jnp.bfloat16)
        hidden[:, 128:512] = active[:, 0:MAIN].astype(jnp.bfloat16)

    def project(r):
        def columns_of(c, carry):
            weight = weights[c // 4, lax.rem(c, 4), :, :, MAIN:PACK].reshape(4 * WROWS, 512)
            columns = pl.ds(pl.multiple_of(c * 4 * WROWS, 128), 4 * WROWS)
            product = lax.dot_general(
                hidden[...], weight, (((1,), (1,)), ((), ())), preferred_element_type=jnp.float32
            )
            down[r, :, :, :, columns] = product.astype(jnp.bfloat16).reshape(8, 2, PART, 4 * WROWS)
            return carry

        lax.fori_loop(0, 8, columns_of, 0)

    def stream(r):
        rows = parts[r]

        def pair(q):
            return partial_ref[q, core, rows].astype(jnp.float32) + sib1[r, q].astype(jnp.float32)

        s1[r][0].wait_recv()
        q = order[0]
        sib1[r, q] = pair(q).astype(jnp.bfloat16)
        opposites = [
            send(
                sib1.at[r, q, :, halves[way]], opposite.at[r, way],
                r1_send.at[r, way], r1_recv.at[r, way], (above2, below2)[way],
            )
            for way in (0, 1)
        ]
        yield
        finals = []
        for way in (0, 1):
            s1[r][1 + way].wait_recv()
            opposites[way].wait_recv()
            q = order[1 + way]
            total = pair(q)
            moved = total[:, way * HALF:(way + 1) * HALF] + opposite[r, way].astype(jnp.float32)
            kept = total[:, (1 - way) * HALF:(2 - way) * HALF]
            sib1[r, q, :, halves[way]] = moved.astype(jnp.bfloat16)
            sib1[r, q, :, halves[1 - way]] = kept.astype(jnp.bfloat16)
            finals.append(send(
                sib1.at[r, q], pairs.at[r, way],
                r1_send.at[r, 2 + way], r1_recv.at[r, 2 + way], (above2, below2)[way],
            ))
        yield
        s1[r][3].wait_recv()
        for copy in finals:
            copy.wait_recv()
        if r == 0:
            fetch_resid.wait()
        branch = (
            pair(z_hi) + pairs[r, 0].astype(jnp.float32) + pairs[r, 1].astype(jnp.float32)
        )
        value = resid_rows[rows].astype(jnp.float32) + modulation_ref[0:1] * branch
        state[r] = value
        average = jnp.mean(value, axis=-1, keepdims=True)
        centered = value - average
        variance = jnp.mean(centered * centered, axis=-1, keepdims=True)
        normal_form = centered * lax.rsqrt(variance + 1e-06)
        normed[r, z, core] = (
            normal_form * (1.0 + modulation_ref[2:3]) + modulation_ref[1:2]
        ).astype(jnp.bfloat16)

        gathered = []

        def to_sibling(view, index):
            gathered.append(send(
                view, view, agsib_send.at[r, index], agsib_recv.at[r, index], sibling
            ))

        def hop(way, step):
            view = normed.at[r, shard((1 - step) * (1 - 2 * way)), core]
            if step == 4:
                view = view.at[:, halves[way]]
            return send(
                view, view, ag_send.at[r, way, step - 1], ag_recv.at[r, way, step - 1],
                (above, below)[way],
            )

        hops = [hop(0, 1), hop(1, 1)]
        to_sibling(normed.at[r, z, core], 0)
        yield
        for step in (1, 2, 3, 4):
            for way in (0, 1):
                hops[way].wait_recv()
                view = normed.at[r, shard(-step * (1 - 2 * way)), core]
                if step < 4:
                    hops[way] = hop(way, step + 1)
                else:
                    view = view.at[:, halves[way]]
                to_sibling(view, 1 + (step - 1) * 2 + way)
            yield
        for copy in gathered:
            copy.wait_recv()
        weights_here()
        up(r)
        project(r)
        s2 = {}
        for i, distance in enumerate((4, 3, -3, 2, -2, 1, -1, 0)):
            q = shard(distance)
            s2[distance] = send(
                down.at[r, q, 1 - core], sib2.at[r, q], s2_send.at[r, i], s2_recv.at[r, i], sibling
            )
        yield

        def pair2(q):
            return down[r, q, core].astype(jnp.float32) + sib2[r, q].astype(jnp.float32)

        sums = [None, None]
        for step in (1, 2, 3, 4):
            for way in (0, 1):
                distance = (5 - step) * (1 - 2 * way)
                q = shard(distance)
                if step == 1:
                    if way == 0:
                        s2[4].wait_recv()
                        sib2[r, q] = pair2(q).astype(jnp.bfloat16)
                    source = sib2.at[r, q, :, halves[way]]
                    target = ring.at[r, way, 0, :, halves[way]]
                else:
                    s2[distance].wait_recv()
                    total = pair2(q)
                    sums[way].wait_recv()
                    if step == 2:
                        moved = (
                            total[:, way * HALF:(way + 1) * HALF]
                            + ring[r, way, 0, :, halves[way]].astype(jnp.float32)
                        )
                        kept = total[:, (1 - way) * HALF:(2 - way) * HALF]
                        sib2[r, q, :, halves[way]] = moved.astype(jnp.bfloat16)
                        sib2[r, q, :, halves[1 - way]] = kept.astype(jnp.bfloat16)
                    else:
                        total = total + ring[r, way, step - 2].astype(jnp.float32)
                        sib2[r, q] = total.astype(jnp.bfloat16)
                    source, target = sib2.at[r, q], ring.at[r, way, step - 1]
                sums[way] = send(
                    source, target, r2_send.at[r, way, step - 1], r2_recv.at[r, way, step - 1],
                    (above, below)[way],
                )
            yield
        s2[0].wait_recv()
        ffn = pair2(z)
        for way in (0, 1):
            sums[way].wait_recv()
            ffn = ffn + ring[r, way, 3].astype(jnp.float32)
        out_ref[rows] = (state[r] + modulation_ref[3:4] * ffn).astype(jnp.bfloat16)
        yield

    stages = 13
    streams = [stream(r) for r in range(STREAMS)]
    for tick in range(stages + LAG * (STREAMS - 1)):
        for r in range(STREAMS):
            if 0 <= tick - LAG * r < stages:
                next(streams[r])
        if tick == 0:
            weights_first()
        if tick == 2:
            weights_second()

    for copy in started:
        copy.wait_send()


def feed_forward(partial_value, resid, modulation, up_weight, down_rows):
    dma = pltpu.SemaphoreType.DMA
    bf16 = jnp.bfloat16
    return pl.pallas_call(
        feed_forward_kernel,
        out_shape=jax.ShapeDtypeStruct((ROWS, D), bf16),
        in_specs=[
            pl.BlockSpec(memory_space=pltpu.VMEM),
            pl.BlockSpec(memory_space=pl.ANY),
            pl.BlockSpec(memory_space=pltpu.VMEM),
            pl.BlockSpec(memory_space=pltpu.VMEM),
            pl.BlockSpec(memory_space=pltpu.VMEM),
        ],
        out_specs=pl.BlockSpec(memory_space=pltpu.VMEM),
        scratch_shapes=[
            pltpu.VMEM((2, 4, 4, WROWS, PACK), bf16),
            pltpu.VMEM((WROWS, PACK), bf16),
            pltpu.VMEM((STREAMS, 4, PART, D), bf16),
            pltpu.VMEM((STREAMS, 2, PART, HALF), bf16),
            pltpu.VMEM((STREAMS, 2, PART, D), bf16),
            pltpu.VMEM((STREAMS, PART, D), jnp.float32),
            pltpu.VMEM((ROWS, D), bf16),
            pltpu.VMEM((STREAMS, 8, 2, PART, D), bf16),
            pltpu.VMEM((16 * PART, 512), bf16),
            pltpu.VMEM((STREAMS, 8, 2, PART, D), bf16),
            pltpu.VMEM((STREAMS, 8, PART, D), bf16),
            pltpu.VMEM((STREAMS, 2, 4, PART, D), bf16),
            dma((1,)), dma((13,)), dma((13,)),
            dma((STREAMS, 4)), dma((STREAMS, 4)), dma((STREAMS, 4)), dma((STREAMS, 4)),
            dma((STREAMS, 2, 4)), dma((STREAMS, 2, 4)), dma((STREAMS, 9)), dma((STREAMS, 9)),
            dma((STREAMS, 8)), dma((STREAMS, 8)), dma((STREAMS, 2, 4)), dma((STREAMS, 2, 4)),
        ],
        compiler_params=pltpu.CompilerParams(
            collective_id=1, has_side_effects=True, vmem_limit_bytes=58 * MIB
        ),
        name="feed_forward",
    )(partial_value, resid, modulation, up_weight, down_rows)


def shards(resid, qkv, band, out_weight, modulation, up_weight, down_weight):
    partial_value = attention(jnp.transpose(qkv, (1, 0, 2)), band, out_weight)
    return feed_forward(
        partial_value.reshape(4, 2, ROWS, D), resid, modulation, up_weight, jnp.transpose(down_weight)
    )


def solution(mesh):
    in_specs = (
        P("frame", None),
        P(("frame", "head"), None, None),
        P("frame", None),
        P("head", None),
        P(),
        P("frame", "head"),
        P("head", "frame"),
    )
    out_specs = P(("frame", "head"), None)
    return jax.shard_map(shards, mesh=mesh, in_specs=in_specs, out_specs=out_specs, check_vma=False)
```

```python
import functools
import math

import jax
import jax.numpy as jnp
from jax import lax
from jax.experimental import pallas as pl
from jax.experimental.pallas import tpu as pltpu
from jax.sharding import PartitionSpec as P

HD = 128
SLOTS = 9
BLOCK = 384
NBLK = 32
N_HEAD = 8
ROWS = BLOCK // N_HEAD
GROUP = 5
INNER = GROUP * HD
D = 5120
MESH = pl.DeviceIdType.MESH
MIB = 2**20

partner_offsets = (0, -8, -4, -2, -1, 1, 2, 4, 8)
VIA = "via"
SLOT = {offset: slot for slot, offset in enumerate(partner_offsets)}
QUERY_ROWS = 128
SCALE_LOG2 = math.log2(math.e) / math.sqrt(HD)
HALF = D // 2
UNITS = 432
MAIN = 384
TAIL = UNITS - MAIN
PACK = 896
WROWS = 160
STREAMS = 3
PART = ROWS // STREAMS
LAG = 1


def layer_kernel(
    qkv_ref, band_ref, out_weight_ref, resid_ref, modulation_ref, up_ref, down_rows_ref, out_ref,
    heads, via, attended, partial_ref,
    weights, other_pack, sib1, opposite, pairs, state, resid_rows, normed, hidden, down, sib2, ring,
    a2a_send, a2a_recv, own_sem, halo_send, halo_recv, weight_sem,
    local_sem, w_send, w_recv, s1_send, s1_recv, r1_send, r1_recv,
    ag_send, ag_recv, agsib_send, agsib_recv, s2_send, s2_recv, r2_send, r2_recv,
):
    me = lax.axis_index("head")
    frame = lax.axis_index("frame")
    block = frame
    z_hi, core = me // 2, lax.rem(me, 2)
    z_lo, yx = frame // 16, lax.rem(frame, 16)
    y, x = yx // 4, lax.rem(yx, 4)
    z = z_hi * 2 + z_lo
    row_start = frame - x
    halves = (pl.ds(0, HALF), pl.ds(HALF, HALF))

    def z_device(other):
        return {"head": (other // 2) * 2 + core, "frame": lax.rem(other, 2) * 16 + yx}

    sibling = {"head": z_hi * 2 + 1 - core, "frame": frame}
    above, below = z_device(lax.rem(z + 1, 8)), z_device(lax.rem(z + 7, 8))
    above2, below2 = z_device(lax.rem(z + 2, 8)), z_device(lax.rem(z + 6, 8))
    x_peers = [{"head": me, "frame": z_lo * 16 + y * 4 + lax.rem(x + k, 4)} for k in (1, 2, 3)]
    y_peers = [{"head": me, "frame": z_lo * 16 + lax.rem(y + k, 4) * 4 + x} for k in (1, 2, 3)]
    other_plane = z_device(z + 1 - 2 * z_lo)

    barrier = pltpu.get_barrier_semaphore()
    greeted = [above, below] + x_peers + y_peers
    greeted += [{"head": lax.rem(me + k, N_HEAD), "frame": frame} for k in range(1, N_HEAD)]
    greeted += [{"head": me, "frame": lax.rem(frame + k, NBLK)} for k in (4, 12, 16, 20, NBLK - 4)]
    for device in greeted:
        pl.semaphore_signal(barrier, inc=1, device_id=device, device_id_type=MESH)

    my_rows = pl.ds(pl.multiple_of(me * ROWS, 16), ROWS)
    fetch_resid = pltpu.make_async_copy(resid_ref.at[my_rows], resid_rows, local_sem.at[0])
    fetch_resid.start()

    lane = lax.broadcasted_iota(jnp.int32, (WROWS, 128), 1)
    blank = jnp.zeros((WROWS, 128 - 2 * TAIL), jnp.float32)
    tails = [
        jnp.concatenate([ref[:, 2 * MAIN:].astype(jnp.float32), blank], axis=1)
        for ref in (up_ref, down_rows_ref)
    ]
    up_tail = [tails[0], pltpu.roll(tails[0], 128 - TAIL, 1)]
    down_tail = [pltpu.roll(tails[1], TAIL, 1), tails[1]]
    mixed_tail = []
    for side in (0, 1):
        down_part = jnp.where(lane < 2 * TAIL, down_tail[side], 0.0)
        mixed_tail.append(jnp.where(lane < TAIL, up_tail[side], down_part))

    def pack(target, side):
        columns = pl.ds(pl.multiple_of(side * MAIN, 128), MAIN)
        target[:, 0:MAIN] = up_ref[:, columns]
        target[:, MAIN:512] = jnp.where(side == 0, mixed_tail[0], mixed_tail[1]).astype(jnp.bfloat16)
        target[:, 512:PACK] = down_rows_ref[:, columns]

    pack(other_pack, 1 - z_lo)
    pack(weights.at[z_lo, y, x], z_lo)

    pl.semaphore_wait(barrier, len(greeted))

    def remote(source, target, send_sem, recv_sem, device):
        return pltpu.make_async_remote_copy(
            source, target, send_sem, recv_sem, device_id=device, device_id_type=MESH
        )

    own_view, other_view = weights.at[z_lo, y, x], weights.at[1 - z_lo, y, x]
    cross = remote(other_pack, own_view, w_send.at[0], w_recv.at[0], other_plane)
    right, left = lax.rem(x + 1, 4), lax.rem(x + 3, 4)
    front, back = lax.rem(y + 1, 4), lax.rem(y + 3, 4)
    to_right, to_left, to_front, to_back = x_peers[0], x_peers[2], y_peers[0], y_peers[2]
    upper, lower = pl.ds(0, WROWS // 2), pl.ds(WROWS // 2, WROWS // 2)
    low, high = pl.ds(0, 2), pl.ds(2, 2)

    def weight_hops(first, hops):
        return [
            remote(view, view, w_send.at[first + i], w_recv.at[first + i], device)
            for i, (view, device) in enumerate(hops)
        ]

    def row_part(row, part):
        return weights.at[z_lo, row, part]

    def column_part(column, part):
        return weights.at[1 - z_lo, part, column]

    piece_near = weight_hops(1, (
        (own_view, to_right), (own_view, to_left), (other_view, to_front), (other_view, to_back),
    ))
    piece_far = weight_hops(5, (
        (weights.at[z_lo, y, left, upper], to_right), (weights.at[z_lo, y, right, lower], to_left),
        (weights.at[1 - z_lo, back, x, upper], to_front), (weights.at[1 - z_lo, front, x, lower], to_back),
    ))
    line_first = weight_hops(9, (
        (row_part(y, low), to_front), (row_part(y, high), to_back),
        (column_part(x, low), to_right), (column_part(x, high), to_left),
    ))
    line_then = weight_hops(13, (
        (row_part(y, high), to_front), (row_part(y, low), to_back),
        (column_part(x, high), to_right), (column_part(x, low), to_left),
    ))
    line_far = weight_hops(17, (
        (row_part(back, low), to_front), (row_part(front, high), to_back),
        (column_part(left, low), to_right), (column_part(right, high), to_left),
    ))
    weight_copies = [cross] + piece_near + piece_far + line_first + line_then + line_far

    def weight_step(landed, sent):
        for copy in landed:
            copy.wait_recv()
        for copy in sent:
            copy.start()

    def frame_device(frame):
        return {"head": me, "frame": frame}

    def head_device(head):
        return {"head": head, "frame": block}

    fetch_weight = pltpu.make_async_copy(out_weight_ref, down.at[0:INNER // PART], weight_sem)

    def to_peer(j, k):
        peer = lax.rem(me + k, N_HEAD)
        columns = pl.ds(pl.multiple_of(peer * INNER + j * HD, HD), HD)
        return pltpu.make_async_remote_copy(
            qkv_ref.at[:, :, columns], heads.at[j, :, 0, my_rows],
            a2a_send.at[j, k - 1], a2a_recv.at[j, k - 1],
            device_id=head_device(peer), device_id_type=MESH,
        )

    def own_piece(j):
        columns = pl.ds(pl.multiple_of(me * INNER + j * HD, HD), HD)
        return pltpu.make_async_copy(
            qkv_ref.at[:, :, columns], heads.at[j, :, 0, my_rows], own_sem.at[j]
        )

    def send_heads(j, carry):
        for k in (4, 3, 5, 2, 6, 1, 7):
            to_peer(j, k).start()
        own_piece(j).start()
        return carry

    lax.fori_loop(0, 2, send_heads, 0)
    cross.start()
    fetch_weight.start()

    low4, high4 = block >= 4, block < NBLK - 4
    both = slice(1, 3)
    routes = (
        (1, 0, -4, block + 4, high4, both),
        (1, 0, 4, block - 4, low4, both),
        (1, 0, -1, block + 1, x < 3, both),
        (1, 0, 1, block - 1, x > 0, both),
        (2, -4, -8, block + 4, low4 & high4 & (block // 4 != 3), both),
        (2, 4, 8, block - 4, low4 & high4 & (block // 4 != 4), both),
        (2, -4, VIA, block - 12, block // 4 == 3, both),
        (2, 4, VIA, block + 12, block // 4 == 4, both),
        (3, VIA, -8, block + 16, block // 4 == 0, both),
        (3, VIA, 8, block - 16, block // 4 == 7, both),
        (2, -4, -1, row_start, (x == 3) & low4, both),
        (2, 4, 1, row_start + 3, (x == 0) & high4, both),
        (2, -1, -2, block + 1, (x == 1) | (x == 2), both),
        (2, 1, 2, block - 1, (x == 1) | (x == 2), both),
        (2, -4, -2, row_start, (x == 2) & low4, both),
        (2, 4, 2, row_start + 3, (x == 1) & high4, both),
        (3, -1, -2, block + 1, (x == 0) & low4, both),
        (3, 1, 2, block - 1, (x == 3) & high4, both),
    )
    arrivals = (
        (2, -4, low4, both),
        (2, 4, high4, both),
        (2, -1, x > 0, both),
        (2, 1, x < 3, both),
        (3, VIA, (block // 4 == 0) | (block // 4 == 7), both),
        (3, -1, (x == 0) & low4, both),
        (3, 1, (x == 3) & high4, both),
        (4, 2, block < NBLK - 2, both),
        (4, -2, block >= 2, both),
        (4, -8, block >= 8, both),
        (4, 8, block < NBLK - 8, both),
    )

    def place(j, slot, part):
        return via.at[j] if slot == VIA else heads.at[j, part, SLOT[slot]]

    def halo_sem(slot):
        return SLOTS - 1 if slot == VIA else SLOT[slot] - 1

    def route_copy(j, index):
        _, source, target, frame_to, _, part = routes[index]
        return pltpu.make_async_remote_copy(
            place(j, source, part), place(j, target, part),
            halo_send.at[j, index], halo_recv.at[j, halo_sem(target)],
            device_id=frame_device(jnp.clip(frame_to, 0, NBLK - 1)), device_id_type=MESH,
        )

    def send_stage(j, stage):
        for index, route in enumerate(routes):
            if route[0] == stage:
                @pl.when(route[4])
                def _():
                    route_copy(j, index).start()

    def wait_stage(j, stage):
        for before, slot, when, part in arrivals:
            if before == stage:
                @pl.when(when)
                def _():
                    landed = place(j, slot, part)
                    pltpu.make_async_copy(landed, landed, halo_recv.at[j, halo_sem(slot)]).wait()

    for offset in partner_offsets[1:]:
        partner = block + offset

        @pl.when((partner < 0) | (partner >= NBLK))
        def _():
            heads[:, 1:3, SLOT[offset]] = jnp.zeros((GROUP, 2, BLOCK, HD), jnp.bfloat16)

    def attend(j):
        widths = []
        for slot, offset in enumerate(partner_offsets):
            partner = block + offset
            present = (partner >= 0) & (partner < NBLK)
            widths.append(jnp.where(present, band_ref[0, slot], 0))
        keys = heads[j, 1].reshape(SLOTS * BLOCK, HD)
        values = heads[j, 2].reshape(SLOTS * BLOCK, HD)
        columns = pl.ds(pl.multiple_of(j * HD, HD), HD)
        for first in range(0, BLOCK, QUERY_ROWS):
            queries = heads[j, 0, 0, first:first + QUERY_ROWS]
            scores = lax.dot_general(
                queries, keys, (((1,), (1,)), ((), ())), preferred_element_type=jnp.float32
            )
            row = lax.broadcasted_iota(jnp.int32, (QUERY_ROWS, BLOCK), 0) + first
            column = lax.broadcasted_iota(jnp.int32, (QUERY_ROWS, BLOCK), 1)
            distance = jnp.abs(row - column)
            parts = []
            for slot in range(SLOTS):
                part = scores[:, slot * BLOCK:(slot + 1) * BLOCK]
                parts.append(jnp.where(distance < widths[slot], part, -1e30))
            top = functools.reduce(jnp.maximum, parts)
            row_max = jnp.max(top, axis=1, keepdims=True)
            weights = [jnp.exp2((part - row_max) * SCALE_LOG2) for part in parts]
            denominator = jnp.sum(functools.reduce(jnp.add, weights), axis=1, keepdims=True)
            probabilities = jnp.concatenate([w.astype(jnp.bfloat16) for w in weights], axis=1)
            summed = jnp.dot(probabilities, values, preferred_element_type=jnp.float32)
            attended[first:first + QUERY_ROWS, columns] = (summed / denominator).astype(jnp.bfloat16)

    def step(it, carry):
        @pl.when(it < GROUP)
        def _():
            for k in range(1, N_HEAD):
                origin = lax.rem(me + N_HEAD - k, N_HEAD)
                landed = heads.at[it, :, 0, pl.ds(pl.multiple_of(origin * ROWS, 16), ROWS)]
                pltpu.make_async_copy(landed, landed, a2a_recv.at[it, k - 1]).wait()
            own_piece(it).wait()
            send_stage(it, 1)

        @pl.when(it < GROUP - 2)
        def _():
            send_heads(it + 2, 0)

        @pl.when((it >= 1) & (it < GROUP + 1))
        def _():
            wait_stage(it - 1, 2)
            send_stage(it - 1, 2)

        @pl.when((it >= 2) & (it < GROUP + 2))
        def _():
            wait_stage(it - 2, 3)
            send_stage(it - 2, 3)

        @pl.when(it == GROUP + 2)
        def _():
            weight_step([cross], piece_near)

        @pl.when(it >= 3)
        def _():
            wait_stage(it - 3, 4)
            attend(it - 3)

        return carry

    lax.fori_loop(0, GROUP + 3, step, 0)

    fetch_weight.wait()

    started = []

    def send(source, target, send_sem, recv_sem, device):
        copy = pltpu.make_async_remote_copy(
            source, target, send_sem, recv_sem, device_id=device, device_id_type=MESH
        )
        copy.start()
        started.append(copy)
        return copy

    order = [lax.rem(z_hi + k, 4) for k in (2, 1, 3, 0)]
    parts = [slice(r * PART, (r + 1) * PART) for r in range(STREAMS)]
    s1 = []

    def project_heads(r):
        rows = attended[...].reshape(N_HEAD, STREAMS, PART, INNER)[:, r].reshape(N_HEAD * PART, INNER)

        def columns_of(c, carry):
            columns = pl.ds(pl.multiple_of(c * 512, 512), 512)
            weight = down[0:INNER // PART, :, columns].reshape(INNER, 512)
            product = jnp.dot(rows, weight, preferred_element_type=jnp.float32)
            partial_ref[r, :, :, :, columns] = product.astype(jnp.bfloat16).reshape(4, 2, PART, 512)
            return carry

        lax.fori_loop(0, D // 512, columns_of, 0)
        s1.append([
            send(
                partial_ref.at[r, q, 1 - core], sib1.at[r, q],
                s1_send.at[r, i], s1_recv.at[r, i], sibling,
            )
            for i, q in enumerate(order)
        ])

    def shard(distance):
        return lax.rem(z + distance + 8, 8)

    def up(r):
        rows = normed[r].reshape(16 * PART, D)
        total = None
        for c in range(4):
            weight = weights[c // 2, 2 * (c % 2):2 * (c % 2) + 2, :, :, 0:512].reshape(8 * WROWS, 512)
            product = jnp.dot(
                rows[:, c * 1280:(c + 1) * 1280], weight, preferred_element_type=jnp.float32
            )
            total = product if total is None else total + product
        active = jax.nn.gelu(total, approximate=True)
        place = lax.broadcasted_iota(jnp.int32, (16 * PART, 128), 1)
        tail = pltpu.roll(active[:, MAIN:512], TAIL, 1)
        tail = jnp.where((place >= TAIL) & (place < 2 * TAIL), tail, 0.0)
        hidden[:, 0:128] = tail.astype(jnp.bfloat16)
        hidden[:, 128:512] = active[:, 0:MAIN].astype(jnp.bfloat16)

    def project(r):
        def columns_of(c, carry):
            weight = weights[c // 4, lax.rem(c, 4), :, :, MAIN:PACK].reshape(4 * WROWS, 512)
            columns = pl.ds(pl.multiple_of(c * 4 * WROWS, 128), 4 * WROWS)
            product = lax.dot_general(
                hidden[...], weight, (((1,), (1,)), ((), ())), preferred_element_type=jnp.float32
            )
            down[r * 16:(r + 1) * 16, :, columns] = product.astype(jnp.bfloat16).reshape(16, PART, 4 * WROWS)
            return carry

        lax.fori_loop(0, 8, columns_of, 0)

    def stream(r):
        rows = parts[r]

        def pair(q):
            return partial_ref[r, q, core].astype(jnp.float32) + sib1[r, q].astype(jnp.float32)

        s1[r][0].wait_recv()
        q = order[0]
        sib1[r, q] = pair(q).astype(jnp.bfloat16)
        opposites = [
            send(
                sib1.at[r, q, :, halves[way]], opposite.at[r, way],
                r1_send.at[r, way], r1_recv.at[r, way], (above2, below2)[way],
            )
            for way in (0, 1)
        ]
        yield
        finals = []
        for way in (0, 1):
            s1[r][1 + way].wait_recv()
            opposites[way].wait_recv()
            q = order[1 + way]
            total = pair(q)
            moved = total[:, way * HALF:(way + 1) * HALF] + opposite[r, way].astype(jnp.float32)
            kept = total[:, (1 - way) * HALF:(2 - way) * HALF]
            sib1[r, q, :, halves[way]] = moved.astype(jnp.bfloat16)
            sib1[r, q, :, halves[1 - way]] = kept.astype(jnp.bfloat16)
            finals.append(send(
                sib1.at[r, q], pairs.at[r, way],
                r1_send.at[r, 2 + way], r1_recv.at[r, 2 + way], (above2, below2)[way],
            ))
        yield
        s1[r][3].wait_recv()
        for copy in finals:
            copy.wait_recv()
        if r == 0:
            fetch_resid.wait()
        branch = (
            pair(z_hi) + pairs[r, 0].astype(jnp.float32) + pairs[r, 1].astype(jnp.float32)
        )
        value = resid_rows[rows].astype(jnp.float32) + modulation_ref[0:1] * branch
        state[r] = value
        average = jnp.mean(value, axis=-1, keepdims=True)
        centered = value - average
        variance = jnp.mean(centered * centered, axis=-1, keepdims=True)
        normal_form = centered * lax.rsqrt(variance + 1e-06)
        normed[r, z, core] = (
            normal_form * (1.0 + modulation_ref[2:3]) + modulation_ref[1:2]
        ).astype(jnp.bfloat16)

        gathered = []

        def to_sibling(view, index):
            gathered.append(send(
                view, view, agsib_send.at[r, index], agsib_recv.at[r, index], sibling
            ))

        def hop(way, step):
            view = normed.at[r, shard((1 - step) * (1 - 2 * way)), core]
            if step == 4:
                view = view.at[:, halves[way]]
            return send(
                view, view, ag_send.at[r, way, step - 1], ag_recv.at[r, way, step - 1],
                (above, below)[way],
            )

        hops = [hop(0, 1), hop(1, 1)]
        to_sibling(normed.at[r, z, core], 0)
        yield
        for step in (1, 2, 3, 4):
            for way in (0, 1):
                hops[way].wait_recv()
                view = normed.at[r, shard(-step * (1 - 2 * way)), core]
                if step < 4:
                    hops[way] = hop(way, step + 1)
                else:
                    view = view.at[:, halves[way]]
                to_sibling(view, 1 + (step - 1) * 2 + way)
            yield
        for copy in gathered:
            copy.wait_recv()
        if r == 0:
            weight_step(line_then + line_far, [])
        up(r)
        project(r)
        s2 = {}
        for i, distance in enumerate((4, 3, -3, 2, -2, 1, -1, 0)):
            q = shard(distance)
            s2[distance] = send(
                down.at[r * 16 + q * 2 + 1 - core], sib2.at[r, q], s2_send.at[r, i], s2_recv.at[r, i], sibling
            )
        yield

        def pair2(q):
            return down[r * 16 + q * 2 + core].astype(jnp.float32) + sib2[r, q].astype(jnp.float32)

        sums = [None, None]
        for step in (1, 2, 3, 4):
            for way in (0, 1):
                distance = (5 - step) * (1 - 2 * way)
                q = shard(distance)
                if step == 1:
                    if way == 0:
                        s2[4].wait_recv()
                        sib2[r, q] = pair2(q).astype(jnp.bfloat16)
                    source = sib2.at[r, q, :, halves[way]]
                    target = ring.at[r, way, 0, :, halves[way]]
                else:
                    s2[distance].wait_recv()
                    total = pair2(q)
                    sums[way].wait_recv()
                    if step == 2:
                        moved = (
                            total[:, way * HALF:(way + 1) * HALF]
                            + ring[r, way, 0, :, halves[way]].astype(jnp.float32)
                        )
                        kept = total[:, (1 - way) * HALF:(2 - way) * HALF]
                        sib2[r, q, :, halves[way]] = moved.astype(jnp.bfloat16)
                        sib2[r, q, :, halves[1 - way]] = kept.astype(jnp.bfloat16)
                    else:
                        total = total + ring[r, way, step - 2].astype(jnp.float32)
                        sib2[r, q] = total.astype(jnp.bfloat16)
                    source, target = sib2.at[r, q], ring.at[r, way, step - 1]
                sums[way] = send(
                    source, target, r2_send.at[r, way, step - 1], r2_recv.at[r, way, step - 1],
                    (above, below)[way],
                )
            yield
        s2[0].wait_recv()
        ffn = pair2(z)
        for way in (0, 1):
            sums[way].wait_recv()
            ffn = ffn + ring[r, way, 3].astype(jnp.float32)
        out_ref[rows] = (state[r] + modulation_ref[3:4] * ffn).astype(jnp.bfloat16)
        yield

    stages = 13
    streams = [stream(r) for r in range(STREAMS)]
    weight_step(piece_near, piece_far)
    project_heads(0)
    project_heads(1)
    weight_step(piece_far, line_first + line_then)
    for tick in range(stages + LAG * (STREAMS - 1)):
        for r in range(STREAMS):
            if 0 <= tick - LAG * r < stages:
                next(streams[r])
        if tick == 0:
            project_heads(2)
        if tick == 2:
            weight_step(line_first, line_far)

    for copy in started + weight_copies:
        copy.wait_send()
    def finish(j, carry):
        for k in range(1, N_HEAD):
            to_peer(j, k).wait_send()
        for index, route in enumerate(routes):
            @pl.when(route[4])
            def _():
                route_copy(j, index).wait_send()
        return carry

    lax.fori_loop(0, GROUP, finish, 0)


def layer(qkv, band, out_weight, resid, modulation, up_weight, down_rows):
    dma = pltpu.SemaphoreType.DMA
    bf16 = jnp.bfloat16
    anywhere, vmem = pl.BlockSpec(memory_space=pl.ANY), pl.BlockSpec(memory_space=pltpu.VMEM)
    return pl.pallas_call(
        layer_kernel,
        out_shape=jax.ShapeDtypeStruct((ROWS, D), bf16),
        in_specs=[
            anywhere, pl.BlockSpec(memory_space=pltpu.SMEM), anywhere, anywhere, vmem, vmem, vmem,
        ],
        out_specs=vmem,
        scratch_shapes=[
            pltpu.VMEM((GROUP, 3, SLOTS, BLOCK, HD), bf16),
            pltpu.VMEM((GROUP, 2, BLOCK, HD), bf16),
            pltpu.VMEM((BLOCK, INNER), bf16),
            pltpu.VMEM((STREAMS, 4, 2, PART, D), bf16),
            pltpu.VMEM((2, 4, 4, WROWS, PACK), bf16),
            pltpu.VMEM((WROWS, PACK), bf16),
            pltpu.VMEM((STREAMS, 4, PART, D), bf16),
            pltpu.VMEM((STREAMS, 2, PART, HALF), bf16),
            pltpu.VMEM((STREAMS, 2, PART, D), bf16),
            pltpu.VMEM((STREAMS, PART, D), jnp.float32),
            pltpu.VMEM((ROWS, D), bf16),
            pltpu.VMEM((STREAMS, 8, 2, PART, D), bf16),
            pltpu.VMEM((16 * PART, 512), bf16),
            pltpu.VMEM((STREAMS * 16, PART, D), bf16),
            pltpu.VMEM((STREAMS, 8, PART, D), bf16),
            pltpu.VMEM((STREAMS, 2, 4, PART, D), bf16),
            dma((GROUP, N_HEAD - 1)), dma((GROUP, N_HEAD - 1)), dma((GROUP,)),
            dma((GROUP, 18)), dma((GROUP, SLOTS)), dma,
            dma((1,)), dma((21,)), dma((21,)),
            dma((STREAMS, 4)), dma((STREAMS, 4)), dma((STREAMS, 4)), dma((STREAMS, 4)),
            dma((STREAMS, 2, 4)), dma((STREAMS, 2, 4)), dma((STREAMS, 9)), dma((STREAMS, 9)),
            dma((STREAMS, 8)), dma((STREAMS, 8)), dma((STREAMS, 2, 4)), dma((STREAMS, 2, 4)),
        ],
        compiler_params=pltpu.CompilerParams(
            collective_id=0, has_side_effects=True, vmem_limit_bytes=62 * MIB
        ),
        name="layer",
    )(qkv, band, out_weight, resid, modulation, up_weight, down_rows)


def shards(resid, qkv, band, out_weight, modulation, up_weight, down_weight):
    return layer(
        jnp.transpose(qkv, (1, 0, 2)), band, out_weight.reshape(INNER // PART, PART, D),
        resid, modulation, up_weight, jnp.transpose(down_weight),
    )


def solution(mesh):
    in_specs = (
        P("frame", None),
        P(("frame", "head"), None, None),
        P("frame", None),
        P("head", None),
        P(),
        P("frame", "head"),
        P("head", "frame"),
    )
    out_specs = P(("frame", "head"), None)
    return jax.shard_map(shards, mesh=mesh, in_specs=in_specs, out_specs=out_specs, check_vma=False)
```

```python
import functools
import math

import jax
import jax.numpy as jnp
from jax import lax
from jax.experimental import pallas as pl
from jax.experimental.pallas import tpu as pltpu
from jax.sharding import PartitionSpec as P

HD = 128
SLOTS = 9
BLOCK = 384
NBLK = 32
N_HEAD = 8
ROWS = BLOCK // N_HEAD
GROUP = 5
INNER = GROUP * HD
D = 5120
MESH = pl.DeviceIdType.MESH
MIB = 2**20

partner_offsets = (0, -8, -4, -2, -1, 1, 2, 4, 8)
VIA = "via"
SLOT = {offset: slot for slot, offset in enumerate(partner_offsets)}
QUERY_ROWS = 128
SCALE_LOG2 = math.log2(math.e) / math.sqrt(HD)
HALF = D // 2
UNITS = 432
MAIN = 384
TAIL = UNITS - MAIN
PACK = 896
WROWS = 160
STREAMS = 3
PART = ROWS // STREAMS
LAG = 2


def layer_kernel(
    qkv_ref, band_ref, out_weight_ref, resid_ref, modulation_ref, up_ref, down_rows_ref, out_ref,
    heads, via, attended, partial_ref,
    weights, other_pack, sib1, opposite, pairs, state, resid_rows, normed, hidden, down, sib2, ring,
    a2a_send, a2a_recv, own_sem, halo_send, halo_recv, weight_sem,
    local_sem, w_send, w_recv, s1_send, s1_recv, r1_send, r1_recv,
    ag_send, ag_recv, agsib_send, agsib_recv, s2_send, s2_recv, r2_send, r2_recv,
):
    me = lax.axis_index("head")
    frame = lax.axis_index("frame")
    block = frame
    z_hi, core = me // 2, lax.rem(me, 2)
    z_lo, yx = frame // 16, lax.rem(frame, 16)
    y, x = yx // 4, lax.rem(yx, 4)
    z = z_hi * 2 + z_lo
    row_start = frame - x
    halves = (pl.ds(0, HALF), pl.ds(HALF, HALF))

    def z_device(other):
        return {"head": (other // 2) * 2 + core, "frame": lax.rem(other, 2) * 16 + yx}

    sibling = {"head": z_hi * 2 + 1 - core, "frame": frame}
    above, below = z_device(lax.rem(z + 1, 8)), z_device(lax.rem(z + 7, 8))
    above2, below2 = z_device(lax.rem(z + 2, 8)), z_device(lax.rem(z + 6, 8))
    x_peers = [{"head": me, "frame": z_lo * 16 + y * 4 + lax.rem(x + k, 4)} for k in (1, 2, 3)]
    y_peers = [{"head": me, "frame": z_lo * 16 + lax.rem(y + k, 4) * 4 + x} for k in (1, 2, 3)]
    other_plane = z_device(z + 1 - 2 * z_lo)

    barrier = pltpu.get_barrier_semaphore()
    greeted = [above, below] + x_peers + y_peers
    greeted += [{"head": lax.rem(me + k, N_HEAD), "frame": frame} for k in range(1, N_HEAD)]
    greeted += [{"head": me, "frame": lax.rem(frame + k, NBLK)} for k in (4, 12, 16, 20, NBLK - 4)]
    for device in greeted:
        pl.semaphore_signal(barrier, inc=1, device_id=device, device_id_type=MESH)

    my_rows = pl.ds(pl.multiple_of(me * ROWS, 16), ROWS)
    fetch_resid = pltpu.make_async_copy(resid_ref.at[my_rows], resid_rows, local_sem.at[0])
    fetch_resid.start()

    lane = lax.broadcasted_iota(jnp.int32, (WROWS, 128), 1)
    blank = jnp.zeros((WROWS, 128 - 2 * TAIL), jnp.float32)
    tails = [
        jnp.concatenate([ref[:, 2 * MAIN:].astype(jnp.float32), blank], axis=1)
        for ref in (up_ref, down_rows_ref)
    ]
    up_tail = [tails[0], pltpu.roll(tails[0], 128 - TAIL, 1)]
    down_tail = [pltpu.roll(tails[1], TAIL, 1), tails[1]]
    mixed_tail = []
    for side in (0, 1):
        down_part = jnp.where(lane < 2 * TAIL, down_tail[side], 0.0)
        mixed_tail.append(jnp.where(lane < TAIL, up_tail[side], down_part))

    def pack(target, side):
        columns = pl.ds(pl.multiple_of(side * MAIN, 128), MAIN)
        target[:, 0:MAIN] = up_ref[:, columns]
        target[:, MAIN:512] = jnp.where(side == 0, mixed_tail[0], mixed_tail[1]).astype(jnp.bfloat16)
        target[:, 512:PACK] = down_rows_ref[:, columns]

    pack(other_pack, 1 - z_lo)
    pack(weights.at[z_lo, y, x], z_lo)

    pl.semaphore_wait(barrier, len(greeted))

    def remote(source, target, send_sem, recv_sem, device):
        return pltpu.make_async_remote_copy(
            source, target, send_sem, recv_sem, device_id=device, device_id_type=MESH
        )

    own_view, other_view = weights.at[z_lo, y, x], weights.at[1 - z_lo, y, x]
    cross = remote(other_pack, own_view, w_send.at[0], w_recv.at[0], other_plane)
    right, left = lax.rem(x + 1, 4), lax.rem(x + 3, 4)
    front, back = lax.rem(y + 1, 4), lax.rem(y + 3, 4)
    to_right, to_left, to_front, to_back = x_peers[0], x_peers[2], y_peers[0], y_peers[2]
    upper, lower = pl.ds(0, WROWS // 2), pl.ds(WROWS // 2, WROWS // 2)
    low, high = pl.ds(0, 2), pl.ds(2, 2)

    def weight_hops(first, hops):
        return [
            remote(view, view, w_send.at[first + i], w_recv.at[first + i], device)
            for i, (view, device) in enumerate(hops)
        ]

    def row_part(row, part):
        return weights.at[z_lo, row, part]

    def column_part(column, part):
        return weights.at[1 - z_lo, part, column]

    piece_near = weight_hops(1, (
        (own_view, to_right), (own_view, to_left), (other_view, to_front), (other_view, to_back),
    ))
    piece_far = weight_hops(5, (
        (weights.at[z_lo, y, left, upper], to_right), (weights.at[z_lo, y, right, lower], to_left),
        (weights.at[1 - z_lo, back, x, upper], to_front), (weights.at[1 - z_lo, front, x, lower], to_back),
    ))
    line_first = weight_hops(9, (
        (row_part(y, low), to_front), (row_part(y, high), to_back),
        (column_part(x, low), to_right), (column_part(x, high), to_left),
    ))
    line_then = weight_hops(13, (
        (row_part(y, high), to_front), (row_part(y, low), to_back),
        (column_part(x, high), to_right), (column_part(x, low), to_left),
    ))
    line_far = weight_hops(17, (
        (row_part(back, low), to_front), (row_part(front, high), to_back),
        (column_part(left, low), to_right), (column_part(right, high), to_left),
    ))
    weight_copies = [cross] + piece_near + piece_far + line_first + line_then + line_far

    def weight_step(landed, sent):
        for copy in landed:
            copy.wait_recv()
        for copy in sent:
            copy.start()

    def frame_device(frame):
        return {"head": me, "frame": frame}

    def head_device(head):
        return {"head": head, "frame": block}

    fetch_weight = pltpu.make_async_copy(out_weight_ref, down.at[0:INNER // PART], weight_sem)

    def to_peer(j, k):
        peer = lax.rem(me + k, N_HEAD)
        columns = pl.ds(pl.multiple_of(peer * INNER + j * HD, HD), HD)
        return pltpu.make_async_remote_copy(
            qkv_ref.at[:, :, columns], heads.at[j, :, 0, my_rows],
            a2a_send.at[j, k - 1], a2a_recv.at[j, k - 1],
            device_id=head_device(peer), device_id_type=MESH,
        )

    def own_piece(j):
        columns = pl.ds(pl.multiple_of(me * INNER + j * HD, HD), HD)
        return pltpu.make_async_copy(
            qkv_ref.at[:, :, columns], heads.at[j, :, 0, my_rows], own_sem.at[j]
        )

    def send_heads(j, carry):
        for k in (4, 3, 5, 2, 6, 1, 7):
            to_peer(j, k).start()
        own_piece(j).start()
        return carry

    lax.fori_loop(0, 2, send_heads, 0)
    for copy in [cross] + piece_near[:2]:
        copy.start()
    fetch_weight.start()

    low4, high4 = block >= 4, block < NBLK - 4
    both, keys_only, values_only = slice(1, 3), slice(1, 2), slice(2, 3)
    routes = (
        (1, 0, -4, block + 4, high4, both),
        (1, 0, 4, block - 4, low4, both),
        (1, 0, -1, block + 1, x < 3, both),
        (1, 0, 1, block - 1, x > 0, both),
        (2, -4, -8, block + 4, low4 & high4 & (block // 4 != 3), both),
        (2, 4, 8, block - 4, low4 & high4 & (block // 4 != 4), both),
        (2, -4, VIA, block - 12, block // 4 == 3, both),
        (2, 4, VIA, block + 12, block // 4 == 4, both),
        (3, VIA, -8, block + 16, block // 4 == 0, both),
        (3, VIA, 8, block - 16, block // 4 == 7, both),
        (2, -4, -1, row_start, (x == 3) & low4, both),
        (2, 4, 1, row_start + 3, (x == 0) & high4, both),
        (2, -1, -2, block + 1, (x == 1) | (x == 2), both),
        (2, 1, 2, block - 1, (x == 1) | (x == 2), both),
        (2, -4, -2, row_start, (x == 2) & low4, keys_only),
        (2, 4, 2, row_start + 3, (x == 1) & high4, keys_only),
        (3, -1, -2, block + 1, (x == 0) & low4, both),
        (3, 1, 2, block - 1, (x == 3) & high4, both),
        (3, 2, -2, block + 4, (x == 0) & high4, values_only),
        (3, -2, 2, block - 4, (x == 3) & low4, values_only),
    )
    arrivals = (
        (2, -4, low4, both),
        (2, 4, high4, both),
        (2, -1, x > 0, both),
        (2, 1, x < 3, both),
        (3, VIA, (block // 4 == 0) | (block // 4 == 7), both),
        (3, -1, (x == 0) & low4, both),
        (3, 1, (x == 3) & high4, both),
        (3, 2, x == 0, both),
        (3, -2, x == 3, both),
        (4, 2, (x != 0) & (x != 3) & (block < NBLK - 2), both),
        (4, -2, (x != 0) & (x != 3) & (block >= 2), both),
        (4, -2, (x == 0) & low4, keys_only),
        (4, -2, (x == 0) & low4, values_only),
        (4, 2, (x == 3) & high4, keys_only),
        (4, 2, (x == 3) & high4, values_only),
        (4, -8, block >= 8, both),
        (4, 8, block < NBLK - 8, both),
    )

    def place(j, slot, part):
        return via.at[j] if slot == VIA else heads.at[j, part, SLOT[slot]]

    def halo_sem(slot, part):
        if part is values_only:
            return SLOTS + (slot > 0)
        return SLOTS - 1 if slot == VIA else SLOT[slot] - 1

    def route_copy(j, index):
        _, source, target, frame_to, _, part = routes[index]
        return pltpu.make_async_remote_copy(
            place(j, source, part), place(j, target, part),
            halo_send.at[j, index], halo_recv.at[j, halo_sem(target, part)],
            device_id=frame_device(jnp.clip(frame_to, 0, NBLK - 1)), device_id_type=MESH,
        )

    def send_stage(j, stage):
        for index, route in enumerate(routes):
            if route[0] == stage:
                @pl.when(route[4])
                def _():
                    route_copy(j, index).start()

    def wait_stage(j, stage):
        for before, slot, when, part in arrivals:
            if before == stage:
                @pl.when(when)
                def _():
                    landed = place(j, slot, part)
                    pltpu.make_async_copy(landed, landed, halo_recv.at[j, halo_sem(slot, part)]).wait()

    for offset in partner_offsets[1:]:
        partner = block + offset

        @pl.when((partner < 0) | (partner >= NBLK))
        def _():
            heads[:, 1:3, SLOT[offset]] = jnp.zeros((GROUP, 2, BLOCK, HD), jnp.bfloat16)

    def attend(j):
        widths = []
        for slot, offset in enumerate(partner_offsets):
            partner = block + offset
            present = (partner >= 0) & (partner < NBLK)
            widths.append(jnp.where(present, band_ref[0, slot], 0))
        keys = heads[j, 1].reshape(SLOTS * BLOCK, HD)
        values = heads[j, 2].reshape(SLOTS * BLOCK, HD)
        columns = pl.ds(pl.multiple_of(j * HD, HD), HD)
        for first in range(0, BLOCK, QUERY_ROWS):
            queries = heads[j, 0, 0, first:first + QUERY_ROWS]
            scores = lax.dot_general(
                queries, keys, (((1,), (1,)), ((), ())), preferred_element_type=jnp.float32
            )
            row = lax.broadcasted_iota(jnp.int32, (QUERY_ROWS, BLOCK), 0) + first
            column = lax.broadcasted_iota(jnp.int32, (QUERY_ROWS, BLOCK), 1)
            distance = jnp.abs(row - column)
            parts = []
            for slot in range(SLOTS):
                part = scores[:, slot * BLOCK:(slot + 1) * BLOCK]
                parts.append(jnp.where(distance < widths[slot], part, -1e30))
            top = functools.reduce(jnp.maximum, parts)
            row_max = jnp.max(top, axis=1, keepdims=True)
            weights = [jnp.exp2((part - row_max) * SCALE_LOG2) for part in parts]
            denominator = jnp.sum(functools.reduce(jnp.add, weights), axis=1, keepdims=True)
            probabilities = jnp.concatenate([w.astype(jnp.bfloat16) for w in weights], axis=1)
            summed = jnp.dot(probabilities, values, preferred_element_type=jnp.float32)
            attended[first:first + QUERY_ROWS, columns] = (summed / denominator).astype(jnp.bfloat16)

    def step(it, carry):
        @pl.when(it < GROUP)
        def _():
            for k in range(1, N_HEAD):
                origin = lax.rem(me + N_HEAD - k, N_HEAD)
                landed = heads.at[it, :, 0, pl.ds(pl.multiple_of(origin * ROWS, 16), ROWS)]
                pltpu.make_async_copy(landed, landed, a2a_recv.at[it, k - 1]).wait()
            own_piece(it).wait()
            send_stage(it, 1)

        @pl.when(it < GROUP - 2)
        def _():
            send_heads(it + 2, 0)

        @pl.when((it >= 1) & (it < GROUP + 1))
        def _():
            wait_stage(it - 1, 2)
            send_stage(it - 1, 2)

        @pl.when((it >= 2) & (it < GROUP + 2))
        def _():
            wait_stage(it - 2, 3)
            send_stage(it - 2, 3)

        @pl.when(it == 1)
        def _():
            weight_step([cross], piece_near[2:])

        @pl.when(it == 2)
        def _():
            weight_step(piece_near, piece_far)

        @pl.when(it == GROUP + 2)
        def _():
            weight_step(piece_far, line_first + line_then)

        @pl.when(it >= 3)
        def _():
            wait_stage(it - 3, 4)
            attend(it - 3)

        return carry

    lax.fori_loop(0, GROUP + 3, step, 0)

    fetch_weight.wait()

    started = []

    def send(source, target, send_sem, recv_sem, device):
        copy = pltpu.make_async_remote_copy(
            source, target, send_sem, recv_sem, device_id=device, device_id_type=MESH
        )
        copy.start()
        started.append(copy)
        return copy

    order = [lax.rem(z_hi + k, 4) for k in (2, 1, 3, 0)]
    parts = [slice(r * PART, (r + 1) * PART) for r in range(STREAMS)]
    s1 = []

    def project_heads(r):
        rows = attended[...].reshape(N_HEAD, STREAMS, PART, INNER)[:, r].reshape(N_HEAD * PART, INNER)

        def columns_of(c, carry):
            columns = pl.ds(pl.multiple_of(c * 512, 512), 512)
            weight = down[0:INNER // PART, :, columns].reshape(INNER, 512)
            product = jnp.dot(rows, weight, preferred_element_type=jnp.float32)
            partial_ref[r, :, :, :, columns] = product.astype(jnp.bfloat16).reshape(4, 2, PART, 512)
            return carry

        lax.fori_loop(0, D // 512, columns_of, 0)
        s1.append([
            send(
                partial_ref.at[r, q, 1 - core], sib1.at[r, q],
                s1_send.at[r, i], s1_recv.at[r, i], sibling,
            )
            for i, q in enumerate(order)
        ])

    def shard(distance):
        return lax.rem(z + distance + 8, 8)

    def up(r):
        rows = normed[r].reshape(16 * PART, D)
        total = None
        for c in range(4):
            weight = weights[c // 2, 2 * (c % 2):2 * (c % 2) + 2, :, :, 0:512].reshape(8 * WROWS, 512)
            product = jnp.dot(
                rows[:, c * 1280:(c + 1) * 1280], weight, preferred_element_type=jnp.float32
            )
            total = product if total is None else total + product
        active = jax.nn.gelu(total, approximate=True)
        place = lax.broadcasted_iota(jnp.int32, (16 * PART, 128), 1)
        tail = pltpu.roll(active[:, MAIN:512], TAIL, 1)
        tail = jnp.where((place >= TAIL) & (place < 2 * TAIL), tail, 0.0)
        hidden[:, 0:128] = tail.astype(jnp.bfloat16)
        hidden[:, 128:512] = active[:, 0:MAIN].astype(jnp.bfloat16)

    def project(r):
        def columns_of(c, carry):
            weight = weights[c // 4, lax.rem(c, 4), :, :, MAIN:PACK].reshape(4 * WROWS, 512)
            columns = pl.ds(pl.multiple_of(c * 4 * WROWS, 128), 4 * WROWS)
            product = lax.dot_general(
                hidden[...], weight, (((1,), (1,)), ((), ())), preferred_element_type=jnp.float32
            )
            down[r * 16:(r + 1) * 16, :, columns] = product.astype(jnp.bfloat16).reshape(16, PART, 4 * WROWS)
            return carry

        lax.fori_loop(0, 8, columns_of, 0)

    def stream(r):
        rows = parts[r]

        def pair(q):
            return partial_ref[r, q, core].astype(jnp.float32) + sib1[r, q].astype(jnp.float32)

        s1[r][0].wait_recv()
        q = order[0]
        sib1[r, q] = pair(q).astype(jnp.bfloat16)
        opposites = [
            send(
                sib1.at[r, q, :, halves[way]], opposite.at[r, way],
                r1_send.at[r, way], r1_recv.at[r, way], (above2, below2)[way],
            )
            for way in (0, 1)
        ]
        yield
        finals = []
        for way in (0, 1):
            s1[r][1 + way].wait_recv()
            opposites[way].wait_recv()
            q = order[1 + way]
            total = pair(q)
            moved = total[:, way * HALF:(way + 1) * HALF] + opposite[r, way].astype(jnp.float32)
            kept = total[:, (1 - way) * HALF:(2 - way) * HALF]
            sib1[r, q, :, halves[way]] = moved.astype(jnp.bfloat16)
            sib1[r, q, :, halves[1 - way]] = kept.astype(jnp.bfloat16)
            finals.append(send(
                sib1.at[r, q], pairs.at[r, way],
                r1_send.at[r, 2 + way], r1_recv.at[r, 2 + way], (above2, below2)[way],
            ))
        yield
        s1[r][3].wait_recv()
        for copy in finals:
            copy.wait_recv()
        if r == 0:
            fetch_resid.wait()
        branch = (
            pair(z_hi) + pairs[r, 0].astype(jnp.float32) + pairs[r, 1].astype(jnp.float32)
        )
        value = resid_rows[rows].astype(jnp.float32) + modulation_ref[0:1] * branch
        state[r] = value
        average = jnp.mean(value, axis=-1, keepdims=True)
        centered = value - average
        variance = jnp.mean(centered * centered, axis=-1, keepdims=True)
        normal_form = centered * lax.rsqrt(variance + 1e-06)
        normed[r, z, core] = (
            normal_form * (1.0 + modulation_ref[2:3]) + modulation_ref[1:2]
        ).astype(jnp.bfloat16)

        gathered = []

        def to_sibling(view, index):
            gathered.append(send(
                view, view, agsib_send.at[r, index], agsib_recv.at[r, index], sibling
            ))

        hops = {}

        def hop(way, step, half):
            view = normed.at[r, shard((1 - step) * (1 - 2 * way)), core, :, halves[half]]
            hops[way, half] = send(
                view, view, ag_send.at[r, way, step - 1, half], ag_recv.at[r, way, step - 1, half],
                (above, below)[way],
            )

        for half in (0, 1):
            for way in (0, 1):
                hop(way, 1, half)
        to_sibling(normed.at[r, z, core], 0)
        yield
        for step in (1, 2, 3, 4):
            for half in (0, 1):
                for way in (0, 1):
                    if step < 4 or half == way:
                        hops[way, half].wait_recv()
                    if step < 3 or step == 3 and half == way:
                        hop(way, step + 1, half)
            for way in (0, 1):
                view = normed.at[r, shard(-step * (1 - 2 * way)), core]
                if step == 4:
                    view = view.at[:, halves[way]]
                to_sibling(view, 1 + (step - 1) * 2 + way)
            yield
        for copy in gathered:
            copy.wait_recv()
        if r == 0:
            weight_step(line_then + line_far, [])
        up(r)
        project(r)
        s2 = {}
        for i, distance in enumerate((4, 3, -3, 2, -2, 1, -1, 0)):
            q = shard(distance)
            s2[distance] = send(
                down.at[r * 16 + q * 2 + 1 - core], sib2.at[r, q], s2_send.at[r, i], s2_recv.at[r, i], sibling
            )
        yield

        def pair2(q, columns):
            return (
                down[r * 16 + q * 2 + core, :, columns].astype(jnp.float32)
                + sib2[r, q, :, columns].astype(jnp.float32)
            )

        sums = {}
        for step in (1, 2, 3, 4):
            for way in (0, 1):
                if step > 1:
                    s2[(5 - step) * (1 - 2 * way)].wait_recv()
                elif way == 0:
                    s2[4].wait_recv()
            for turn in (0, 1):
                for way in (0, 1):
                    half = way if turn else 1 - way
                    if step == 1 and not turn:
                        continue
                    q, columns = shard((5 - step) * (1 - 2 * way)), halves[half]
                    total = pair2(q, columns)
                    if (way, half) in sums:
                        sums[way, half].wait_recv()
                        total = total + ring[r, way, step - 2, :, columns].astype(jnp.float32)
                    sib2[r, q, :, columns] = total.astype(jnp.bfloat16)
                    sums[way, half] = send(
                        sib2.at[r, q, :, columns], ring.at[r, way, step - 1, :, columns],
                        r2_send.at[r, way, step - 1, half], r2_recv.at[r, way, step - 1, half],
                        (above, below)[way],
                    )
            yield
        s2[0].wait_recv()
        for half in (0, 1):
            columns = halves[half]
            ffn = pair2(z, columns)
            for way in (0, 1):
                sums[way, half].wait_recv()
                ffn = ffn + ring[r, way, 3, :, columns].astype(jnp.float32)
            out_ref[rows, columns] = (
                state[r, :, columns] + modulation_ref[3:4, columns] * ffn
            ).astype(jnp.bfloat16)
        yield

    stages = 13
    streams = [stream(r) for r in range(STREAMS)]
    project_heads(0)
    project_heads(1)
    for tick in range(stages + LAG * (STREAMS - 1)):
        for r in range(STREAMS):
            if 0 <= tick - LAG * r < stages:
                next(streams[r])
        if tick == 0:
            project_heads(2)
        if tick == 0:
            weight_step(line_first, line_far)

    for copy in started + weight_copies:
        copy.wait_send()
    def finish(j, carry):
        for k in range(1, N_HEAD):
            to_peer(j, k).wait_send()
        for index, route in enumerate(routes):
            @pl.when(route[4])
            def _():
                route_copy(j, index).wait_send()
        return carry

    lax.fori_loop(0, GROUP, finish, 0)


def layer(qkv, band, out_weight, resid, modulation, up_weight, down_rows):
    dma = pltpu.SemaphoreType.DMA
    bf16 = jnp.bfloat16
    anywhere, vmem = pl.BlockSpec(memory_space=pl.ANY), pl.BlockSpec(memory_space=pltpu.VMEM)
    return pl.pallas_call(
        layer_kernel,
        out_shape=jax.ShapeDtypeStruct((ROWS, D), bf16),
        in_specs=[
            anywhere, pl.BlockSpec(memory_space=pltpu.SMEM), anywhere, anywhere, vmem, vmem, vmem,
        ],
        out_specs=vmem,
        scratch_shapes=[
            pltpu.VMEM((GROUP, 3, SLOTS, BLOCK, HD), bf16),
            pltpu.VMEM((GROUP, 2, BLOCK, HD), bf16),
            pltpu.VMEM((BLOCK, INNER), bf16),
            pltpu.VMEM((STREAMS, 4, 2, PART, D), bf16),
            pltpu.VMEM((2, 4, 4, WROWS, PACK), bf16),
            pltpu.VMEM((WROWS, PACK), bf16),
            pltpu.VMEM((STREAMS, 4, PART, D), bf16),
            pltpu.VMEM((STREAMS, 2, PART, HALF), bf16),
            pltpu.VMEM((STREAMS, 2, PART, D), bf16),
            pltpu.VMEM((STREAMS, PART, D), jnp.float32),
            pltpu.VMEM((ROWS, D), bf16),
            pltpu.VMEM((STREAMS, 8, 2, PART, D), bf16),
            pltpu.VMEM((16 * PART, 512), bf16),
            pltpu.VMEM((STREAMS * 16, PART, D), bf16),
            pltpu.VMEM((STREAMS, 8, PART, D), bf16),
            pltpu.VMEM((STREAMS, 2, 4, PART, D), bf16),
            dma((GROUP, N_HEAD - 1)), dma((GROUP, N_HEAD - 1)), dma((GROUP,)),
            dma((GROUP, 20)), dma((GROUP, SLOTS + 2)), dma,
            dma((1,)), dma((21,)), dma((21,)),
            dma((STREAMS, 4)), dma((STREAMS, 4)), dma((STREAMS, 4)), dma((STREAMS, 4)),
            dma((STREAMS, 2, 4, 2)), dma((STREAMS, 2, 4, 2)), dma((STREAMS, 9)), dma((STREAMS, 9)),
            dma((STREAMS, 8)), dma((STREAMS, 8)), dma((STREAMS, 2, 4, 2)), dma((STREAMS, 2, 4, 2)),
        ],
        compiler_params=pltpu.CompilerParams(
            collective_id=0, has_side_effects=True, vmem_limit_bytes=62 * MIB
        ),
        name="layer",
    )(qkv, band, out_weight, resid, modulation, up_weight, down_rows)


def shards(resid, qkv, band, out_weight, modulation, up_weight, down_weight):
    return layer(
        jnp.transpose(qkv, (1, 0, 2)), band, out_weight.reshape(INNER // PART, PART, D),
        resid, modulation, up_weight, jnp.transpose(down_weight),
    )


def solution(mesh):
    in_specs = (
        P("frame", None),
        P(("frame", "head"), None, None),
        P("frame", None),
        P("head", None),
        P(),
        P("frame", "head"),
        P("head", "frame"),
    )
    out_specs = P(("frame", "head"), None)
    return jax.shard_map(shards, mesh=mesh, in_specs=in_specs, out_specs=out_specs, check_vma=False)
```

```python
import functools
import math

import jax
import jax.numpy as jnp
from jax import lax
from jax.experimental import pallas as pl
from jax.experimental.pallas import tpu as pltpu
from jax.sharding import PartitionSpec as P

HD = 128
SLOTS = 9
BLOCK = 384
NBLK = 32
N_HEAD = 8
ROWS = BLOCK // N_HEAD
GROUP = 5
INNER = GROUP * HD
D = 5120
MESH = pl.DeviceIdType.MESH
MIB = 2**20

partner_offsets = (0, -8, -4, -2, -1, 1, 2, 4, 8)
VIA = "via"
SLOT = {offset: slot for slot, offset in enumerate(partner_offsets)}
QUERY_ROWS = 128
SCALE_LOG2 = math.log2(math.e) / math.sqrt(HD)
HALF = D // 2
UNITS = 432
MAIN = 384
TAIL = UNITS - MAIN
PACK = 896
WROWS = 160
STREAMS = 3
PART = ROWS // STREAMS
LAG = 2


def layer_kernel(
    qkv_ref, band_ref, out_weight_ref, resid_ref, modulation_ref, up_ref, down_rows_ref, out_ref,
    heads, via, attended, partial_ref,
    weights, other_pack, sib1, opposite, pairs, state, resid_rows, normed, hidden, down, sib2, ring,
    a2a_send, a2a_recv, own_sem, halo_send, halo_recv, weight_sem,
    local_sem, w_send, w_recv, s1_send, s1_recv, r1_send, r1_recv,
    ag_send, ag_recv, agsib_send, agsib_recv, s2_send, s2_recv, r2_send, r2_recv,
):
    me = lax.axis_index("head")
    frame = lax.axis_index("frame")
    block = frame
    z_hi, core = me // 2, lax.rem(me, 2)
    z_lo, yx = frame // 16, lax.rem(frame, 16)
    y, x = yx // 4, lax.rem(yx, 4)
    z = z_hi * 2 + z_lo
    row_start = frame - x
    halves = (pl.ds(0, HALF), pl.ds(HALF, HALF))

    def z_device(other):
        return {"head": (other // 2) * 2 + core, "frame": lax.rem(other, 2) * 16 + yx}

    sibling = {"head": z_hi * 2 + 1 - core, "frame": frame}
    above, below = z_device(lax.rem(z + 1, 8)), z_device(lax.rem(z + 7, 8))
    above2, below2 = z_device(lax.rem(z + 2, 8)), z_device(lax.rem(z + 6, 8))
    x_peers = [{"head": me, "frame": z_lo * 16 + y * 4 + lax.rem(x + k, 4)} for k in (1, 2, 3)]
    y_peers = [{"head": me, "frame": z_lo * 16 + lax.rem(y + k, 4) * 4 + x} for k in (1, 2, 3)]
    other_plane = z_device(z + 1 - 2 * z_lo)

    barrier = pltpu.get_barrier_semaphore()
    greeted = [above, below] + x_peers + y_peers
    greeted += [{"head": lax.rem(me + k, N_HEAD), "frame": frame} for k in range(1, N_HEAD)]
    greeted += [{"head": me, "frame": lax.rem(frame + k, NBLK)} for k in (4, 12, 16, 20, NBLK - 4)]
    for device in greeted:
        pl.semaphore_signal(barrier, inc=1, device_id=device, device_id_type=MESH)

    my_rows = pl.ds(pl.multiple_of(me * ROWS, 16), ROWS)
    fetch_resid = pltpu.make_async_copy(resid_ref.at[my_rows], resid_rows, local_sem.at[0])
    fetch_resid.start()

    lane = lax.broadcasted_iota(jnp.int32, (WROWS, 128), 1)
    blank = jnp.zeros((WROWS, 128 - 2 * TAIL), jnp.float32)
    tails = [
        jnp.concatenate([ref[:, 2 * MAIN:].astype(jnp.float32), blank], axis=1)
        for ref in (up_ref, down_rows_ref)
    ]
    up_tail = [tails[0], pltpu.roll(tails[0], 128 - TAIL, 1)]
    down_tail = [pltpu.roll(tails[1], TAIL, 1), tails[1]]
    mixed_tail = []
    for side in (0, 1):
        down_part = jnp.where(lane < 2 * TAIL, down_tail[side], 0.0)
        mixed_tail.append(jnp.where(lane < TAIL, up_tail[side], down_part))

    def pack(target, side):
        columns = pl.ds(pl.multiple_of(side * MAIN, 128), MAIN)
        target[:, 0:MAIN] = up_ref[:, columns]
        target[:, MAIN:512] = jnp.where(side == 0, mixed_tail[0], mixed_tail[1]).astype(jnp.bfloat16)
        target[:, 512:PACK] = down_rows_ref[:, columns]

    pack(other_pack, 1 - z_lo)
    pack(weights.at[z_lo, y, x], z_lo)

    pl.semaphore_wait(barrier, len(greeted))

    def remote(source, target, send_sem, recv_sem, device):
        return pltpu.make_async_remote_copy(
            source, target, send_sem, recv_sem, device_id=device, device_id_type=MESH
        )

    own_view, other_view = weights.at[z_lo, y, x], weights.at[1 - z_lo, y, x]
    cross = remote(other_pack, own_view, w_send.at[0], w_recv.at[0], other_plane)
    right, left = lax.rem(x + 1, 4), lax.rem(x + 3, 4)
    front, back = lax.rem(y + 1, 4), lax.rem(y + 3, 4)
    to_right, to_left, to_front, to_back = x_peers[0], x_peers[2], y_peers[0], y_peers[2]
    upper, lower = pl.ds(0, WROWS // 2), pl.ds(WROWS // 2, WROWS // 2)
    low, high = pl.ds(0, 2), pl.ds(2, 2)

    def weight_hops(first, hops):
        return [
            remote(view, view, w_send.at[first + i], w_recv.at[first + i], device)
            for i, (view, device) in enumerate(hops)
        ]

    def row_part(row, part):
        return weights.at[z_lo, row, part]

    def column_part(column, part):
        return weights.at[1 - z_lo, part, column]

    piece_near = weight_hops(1, (
        (own_view, to_right), (own_view, to_left), (other_view, to_front), (other_view, to_back),
    ))
    piece_far = weight_hops(5, (
        (weights.at[z_lo, y, left, upper], to_right), (weights.at[z_lo, y, right, lower], to_left),
        (weights.at[1 - z_lo, back, x, upper], to_front), (weights.at[1 - z_lo, front, x, lower], to_back),
    ))
    line_first = weight_hops(9, (
        (row_part(y, low), to_front), (row_part(y, high), to_back),
        (column_part(x, low), to_right), (column_part(x, high), to_left),
    ))
    line_then = weight_hops(13, (
        (row_part(y, high), to_front), (row_part(y, low), to_back),
        (column_part(x, high), to_right), (column_part(x, low), to_left),
    ))
    line_far = weight_hops(17, (
        (row_part(back, low), to_front), (row_part(front, high), to_back),
        (column_part(left, low), to_right), (column_part(right, high), to_left),
    ))
    weight_copies = [cross] + piece_near + piece_far + line_first + line_then + line_far

    def weight_step(landed, sent):
        for copy in landed:
            copy.wait_recv()
        for copy in sent:
            copy.start()

    def frame_device(frame):
        return {"head": me, "frame": frame}

    def head_device(head):
        return {"head": head, "frame": block}

    fetch_weight = pltpu.make_async_copy(out_weight_ref, down.at[0:INNER // PART], weight_sem)

    queries_part, halo_part = slice(0, 1), slice(1, 3)

    def to_peer(j, k, part):
        peer = lax.rem(me + k, N_HEAD)
        columns = pl.ds(pl.multiple_of(peer * INNER + j * HD, HD), HD)
        kind = part.start
        return pltpu.make_async_remote_copy(
            qkv_ref.at[part, :, columns], heads.at[j, part, 0, my_rows],
            a2a_send.at[j, k - 1, kind], a2a_recv.at[j, k - 1, kind],
            device_id=head_device(peer), device_id_type=MESH,
        )

    def wait_peers(j, part):
        for k in range(1, N_HEAD):
            origin = lax.rem(me + N_HEAD - k, N_HEAD)
            landed = heads.at[j, part, 0, pl.ds(pl.multiple_of(origin * ROWS, 16), ROWS)]
            pltpu.make_async_copy(landed, landed, a2a_recv.at[j, k - 1, part.start]).wait()

    def own_piece(j):
        columns = pl.ds(pl.multiple_of(me * INNER + j * HD, HD), HD)
        return pltpu.make_async_copy(
            qkv_ref.at[:, :, columns], heads.at[j, :, 0, my_rows], own_sem.at[j]
        )

    def send_heads(j, carry):
        for k in (4, 3, 5, 2, 6, 1, 7):
            to_peer(j, k, halo_part).start()
        own_piece(j).start()
        return carry

    def send_queries(j):
        for k in (4, 3, 5, 2, 6, 1, 7):
            to_peer(j, k, queries_part).start()

    lax.fori_loop(0, 2, send_heads, 0)
    for copy in [cross] + piece_near[:2]:
        copy.start()
    fetch_weight.start()

    low4, high4 = block >= 4, block < NBLK - 4
    both, keys_only, values_only = slice(1, 3), slice(1, 2), slice(2, 3)
    routes = (
        (1, 0, -4, block + 4, high4, both),
        (1, 0, 4, block - 4, low4, both),
        (1, 0, -1, block + 1, x < 3, both),
        (1, 0, 1, block - 1, x > 0, both),
        (2, -4, -8, block + 4, low4 & high4 & (block // 4 != 3), both),
        (2, 4, 8, block - 4, low4 & high4 & (block // 4 != 4), both),
        (2, -4, VIA, block - 12, block // 4 == 3, both),
        (2, 4, VIA, block + 12, block // 4 == 4, both),
        (3, VIA, -8, block + 16, block // 4 == 0, both),
        (3, VIA, 8, block - 16, block // 4 == 7, both),
        (2, -4, -1, row_start, (x == 3) & low4, both),
        (2, 4, 1, row_start + 3, (x == 0) & high4, both),
        (2, -1, -2, block + 1, (x == 1) | (x == 2), both),
        (2, 1, 2, block - 1, (x == 1) | (x == 2), both),
        (2, -4, -2, row_start, (x == 2) & low4, keys_only),
        (2, 4, 2, row_start + 3, (x == 1) & high4, keys_only),
        (3, -1, -2, block + 1, (x == 0) & low4, both),
        (3, 1, 2, block - 1, (x == 3) & high4, both),
        (3, 2, -2, block + 4, (x == 0) & high4, values_only),
        (3, -2, 2, block - 4, (x == 3) & low4, values_only),
    )
    arrivals = (
        (2, -4, low4, both),
        (2, 4, high4, both),
        (2, -1, x > 0, both),
        (2, 1, x < 3, both),
        (3, VIA, (block // 4 == 0) | (block // 4 == 7), both),
        (3, -1, (x == 0) & low4, both),
        (3, 1, (x == 3) & high4, both),
        (3, 2, x == 0, both),
        (3, -2, x == 3, both),
        (4, 2, (x != 0) & (x != 3) & (block < NBLK - 2), both),
        (4, -2, (x != 0) & (x != 3) & (block >= 2), both),
        (4, -2, (x == 0) & low4, keys_only),
        (4, -2, (x == 0) & low4, values_only),
        (4, 2, (x == 3) & high4, keys_only),
        (4, 2, (x == 3) & high4, values_only),
        (4, -8, block >= 8, both),
        (4, 8, block < NBLK - 8, both),
    )

    def place(j, slot, part):
        return via.at[j] if slot == VIA else heads.at[j, part, SLOT[slot]]

    def halo_sem(slot, part):
        if part is values_only:
            return SLOTS + (slot > 0)
        return SLOTS - 1 if slot == VIA else SLOT[slot] - 1

    def route_copy(j, index):
        _, source, target, frame_to, _, part = routes[index]
        return pltpu.make_async_remote_copy(
            place(j, source, part), place(j, target, part),
            halo_send.at[j, index], halo_recv.at[j, halo_sem(target, part)],
            device_id=frame_device(jnp.clip(frame_to, 0, NBLK - 1)), device_id_type=MESH,
        )

    def send_stage(j, stage):
        for index, route in enumerate(routes):
            if route[0] == stage:
                @pl.when(route[4])
                def _():
                    route_copy(j, index).start()

    def wait_stage(j, stage):
        for before, slot, when, part in arrivals:
            if before == stage:
                @pl.when(when)
                def _():
                    landed = place(j, slot, part)
                    pltpu.make_async_copy(landed, landed, halo_recv.at[j, halo_sem(slot, part)]).wait()

    for offset in partner_offsets[1:]:
        partner = block + offset

        @pl.when((partner < 0) | (partner >= NBLK))
        def _():
            heads[:, 1:3, SLOT[offset]] = jnp.zeros((GROUP, 2, BLOCK, HD), jnp.bfloat16)

    def attend(j):
        widths = []
        for slot, offset in enumerate(partner_offsets):
            partner = block + offset
            present = (partner >= 0) & (partner < NBLK)
            widths.append(jnp.where(present, band_ref[0, slot], 0))
        keys = heads[j, 1].reshape(SLOTS * BLOCK, HD)
        values = heads[j, 2].reshape(SLOTS * BLOCK, HD)
        columns = pl.ds(pl.multiple_of(j * HD, HD), HD)
        for first in range(0, BLOCK, QUERY_ROWS):
            queries = heads[j, 0, 0, first:first + QUERY_ROWS]
            scores = lax.dot_general(
                queries, keys, (((1,), (1,)), ((), ())), preferred_element_type=jnp.float32
            )
            row = lax.broadcasted_iota(jnp.int32, (QUERY_ROWS, BLOCK), 0) + first
            column = lax.broadcasted_iota(jnp.int32, (QUERY_ROWS, BLOCK), 1)
            distance = jnp.abs(row - column)
            parts = []
            for slot in range(SLOTS):
                part = scores[:, slot * BLOCK:(slot + 1) * BLOCK]
                parts.append(jnp.where(distance < widths[slot], part, -1e30))
            top = functools.reduce(jnp.maximum, parts)
            row_max = jnp.max(top, axis=1, keepdims=True)
            weights = [jnp.exp2((part - row_max) * SCALE_LOG2) for part in parts]
            denominator = jnp.sum(functools.reduce(jnp.add, weights), axis=1, keepdims=True)
            probabilities = jnp.concatenate([w.astype(jnp.bfloat16) for w in weights], axis=1)
            summed = jnp.dot(probabilities, values, preferred_element_type=jnp.float32)
            attended[first:first + QUERY_ROWS, columns] = (summed / denominator).astype(jnp.bfloat16)

    def step(it, carry):
        @pl.when(it < GROUP)
        def _():
            wait_peers(it, halo_part)
            own_piece(it).wait()
            send_stage(it, 1)

        @pl.when(it < GROUP - 2)
        def _():
            send_heads(it + 2, 0)

        @pl.when(it < GROUP)
        def _():
            send_queries(it)

        @pl.when((it >= 1) & (it < GROUP + 1))
        def _():
            wait_stage(it - 1, 2)
            send_stage(it - 1, 2)

        @pl.when((it >= 2) & (it < GROUP + 2))
        def _():
            wait_stage(it - 2, 3)
            send_stage(it - 2, 3)

        @pl.when(it == 1)
        def _():
            weight_step([cross], piece_near[2:])

        @pl.when(it == 2)
        def _():
            weight_step(piece_near, piece_far)

        @pl.when(it == GROUP + 2)
        def _():
            weight_step(piece_far, [])

        @pl.when(it >= 3)
        def _():
            wait_peers(it - 3, queries_part)
            wait_stage(it - 3, 4)
            attend(it - 3)

        return carry

    lax.fori_loop(0, GROUP + 3, step, 0)

    fetch_weight.wait()

    started = []

    def send(source, target, send_sem, recv_sem, device):
        copy = pltpu.make_async_remote_copy(
            source, target, send_sem, recv_sem, device_id=device, device_id_type=MESH
        )
        copy.start()
        started.append(copy)
        return copy

    order = [lax.rem(z_hi + k, 4) for k in (2, 1, 3, 0)]
    parts = [slice(r * PART, (r + 1) * PART) for r in range(STREAMS)]
    s1 = []

    def project_heads(r):
        rows = attended[...].reshape(N_HEAD, STREAMS, PART, INNER)[:, r].reshape(N_HEAD * PART, INNER)

        def columns_of(c, carry):
            columns = pl.ds(pl.multiple_of(c * 512, 512), 512)
            weight = down[0:INNER // PART, :, columns].reshape(INNER, 512)
            product = jnp.dot(rows, weight, preferred_element_type=jnp.float32)
            partial_ref[r, :, :, :, columns] = product.astype(jnp.bfloat16).reshape(4, 2, PART, 512)
            return carry

        lax.fori_loop(0, D // 512, columns_of, 0)
        s1.append([
            send(
                partial_ref.at[r, q, 1 - core], sib1.at[r, q],
                s1_send.at[r, i], s1_recv.at[r, i], sibling,
            )
            for i, q in enumerate(order)
        ])

    def shard(distance):
        return lax.rem(z + distance + 8, 8)

    def up(r):
        rows = normed[r].reshape(16 * PART, D)
        total = None
        for c in range(4):
            weight = weights[c // 2, 2 * (c % 2):2 * (c % 2) + 2, :, :, 0:512].reshape(8 * WROWS, 512)
            product = jnp.dot(
                rows[:, c * 1280:(c + 1) * 1280], weight, preferred_element_type=jnp.float32
            )
            total = product if total is None else total + product
        active = jax.nn.gelu(total, approximate=True)
        place = lax.broadcasted_iota(jnp.int32, (16 * PART, 128), 1)
        tail = pltpu.roll(active[:, MAIN:512], TAIL, 1)
        tail = jnp.where((place >= TAIL) & (place < 2 * TAIL), tail, 0.0)
        hidden[:, 0:128] = tail.astype(jnp.bfloat16)
        hidden[:, 128:512] = active[:, 0:MAIN].astype(jnp.bfloat16)

    def project(r):
        def columns_of(c, carry):
            weight = weights[c // 4, lax.rem(c, 4), :, :, MAIN:PACK].reshape(4 * WROWS, 512)
            columns = pl.ds(pl.multiple_of(c * 4 * WROWS, 128), 4 * WROWS)
            product = lax.dot_general(
                hidden[...], weight, (((1,), (1,)), ((), ())), preferred_element_type=jnp.float32
            )
            down[r * 16:(r + 1) * 16, :, columns] = product.astype(jnp.bfloat16).reshape(16, PART, 4 * WROWS)
            return carry

        lax.fori_loop(0, 8, columns_of, 0)

    def stream(r):
        rows = parts[r]

        def pair(q):
            return partial_ref[r, q, core].astype(jnp.float32) + sib1[r, q].astype(jnp.float32)

        s1[r][0].wait_recv()
        q = order[0]
        sib1[r, q] = pair(q).astype(jnp.bfloat16)
        opposites = [
            send(
                sib1.at[r, q, :, halves[way]], opposite.at[r, way],
                r1_send.at[r, way], r1_recv.at[r, way], (above2, below2)[way],
            )
            for way in (0, 1)
        ]
        yield
        finals = []
        for way in (0, 1):
            s1[r][1 + way].wait_recv()
            opposites[way].wait_recv()
            q = order[1 + way]
            total = pair(q)
            moved = total[:, way * HALF:(way + 1) * HALF] + opposite[r, way].astype(jnp.float32)
            kept = total[:, (1 - way) * HALF:(2 - way) * HALF]
            sib1[r, q, :, halves[way]] = moved.astype(jnp.bfloat16)
            sib1[r, q, :, halves[1 - way]] = kept.astype(jnp.bfloat16)
            finals.append(send(
                sib1.at[r, q], pairs.at[r, way],
                r1_send.at[r, 2 + way], r1_recv.at[r, 2 + way], (above2, below2)[way],
            ))
        yield
        s1[r][3].wait_recv()
        for copy in finals:
            copy.wait_recv()
        if r == 0:
            fetch_resid.wait()
        branch = (
            pair(z_hi) + pairs[r, 0].astype(jnp.float32) + pairs[r, 1].astype(jnp.float32)
        )
        value = resid_rows[rows].astype(jnp.float32) + modulation_ref[0:1] * branch
        state[r] = value
        average = jnp.mean(value, axis=-1, keepdims=True)
        centered = value - average
        variance = jnp.mean(centered * centered, axis=-1, keepdims=True)
        normal_form = centered * lax.rsqrt(variance + 1e-06)
        normed[r, z, core] = (
            normal_form * (1.0 + modulation_ref[2:3]) + modulation_ref[1:2]
        ).astype(jnp.bfloat16)

        gathered = []

        def to_sibling(view, index):
            gathered.append(send(
                view, view, agsib_send.at[r, index], agsib_recv.at[r, index], sibling
            ))

        hops = {}

        def hop(way, step, half):
            view = normed.at[r, shard((1 - step) * (1 - 2 * way)), core, :, halves[half]]
            hops[way, half] = send(
                view, view, ag_send.at[r, way, step - 1, half], ag_recv.at[r, way, step - 1, half],
                (above, below)[way],
            )

        for half in (0, 1):
            for way in (0, 1):
                hop(way, 1, half)
        to_sibling(normed.at[r, z, core], 0)
        yield
        for step in (1, 2, 3, 4):
            for half in (0, 1):
                for way in (0, 1):
                    if step < 4 or half == way:
                        hops[way, half].wait_recv()
                    if step < 3 or step == 3 and half == way:
                        hop(way, step + 1, half)
            for way in (0, 1):
                view = normed.at[r, shard(-step * (1 - 2 * way)), core]
                if step == 4:
                    view = view.at[:, halves[way]]
                to_sibling(view, 1 + (step - 1) * 2 + way)
            yield
        for copy in gathered:
            copy.wait_recv()
        if r == 0:
            weight_step(line_then + line_far, [])
        up(r)
        project(r)
        s2 = {}
        for i, distance in enumerate((4, 3, -3, 2, -2, 1, -1, 0)):
            q = shard(distance)
            s2[distance] = send(
                down.at[r * 16 + q * 2 + 1 - core], sib2.at[r, q], s2_send.at[r, i], s2_recv.at[r, i], sibling
            )
        yield

        def pair2(q, columns):
            return (
                down[r * 16 + q * 2 + core, :, columns].astype(jnp.float32)
                + sib2[r, q, :, columns].astype(jnp.float32)
            )

        sums = {}
        for step in (1, 2, 3, 4):
            for way in (0, 1):
                if step > 1:
                    s2[(5 - step) * (1 - 2 * way)].wait_recv()
                elif way == 0:
                    s2[4].wait_recv()
            for turn in (0, 1):
                for way in (0, 1):
                    half = way if turn else 1 - way
                    if step == 1 and not turn:
                        continue
                    q, columns = shard((5 - step) * (1 - 2 * way)), halves[half]
                    total = pair2(q, columns)
                    if (way, half) in sums:
                        sums[way, half].wait_recv()
                        total = total + ring[r, way, step - 2, :, columns].astype(jnp.float32)
                    sib2[r, q, :, columns] = total.astype(jnp.bfloat16)
                    sums[way, half] = send(
                        sib2.at[r, q, :, columns], ring.at[r, way, step - 1, :, columns],
                        r2_send.at[r, way, step - 1, half], r2_recv.at[r, way, step - 1, half],
                        (above, below)[way],
                    )
            yield
        s2[0].wait_recv()
        for half in (0, 1):
            columns = halves[half]
            ffn = pair2(z, columns)
            for way in (0, 1):
                sums[way, half].wait_recv()
                ffn = ffn + ring[r, way, 3, :, columns].astype(jnp.float32)
            out_ref[rows, columns] = (
                state[r, :, columns] + modulation_ref[3:4, columns] * ffn
            ).astype(jnp.bfloat16)
        yield

    stages = 13
    streams = [stream(r) for r in range(STREAMS)]
    project_heads(0)
    project_heads(1)
    weight_step([], line_first + line_then)
    for tick in range(stages + LAG * (STREAMS - 1)):
        for r in range(STREAMS):
            if 0 <= tick - LAG * r < stages:
                next(streams[r])
        if tick == 0:
            project_heads(2)
        if tick == 2:
            weight_step(line_first, line_far)

    for copy in started + weight_copies:
        copy.wait_send()
    def finish(j, carry):
        for k in range(1, N_HEAD):
            to_peer(j, k, queries_part).wait_send()
            to_peer(j, k, halo_part).wait_send()
        for index, route in enumerate(routes):
            @pl.when(route[4])
            def _():
                route_copy(j, index).wait_send()
        return carry

    lax.fori_loop(0, GROUP, finish, 0)


def layer(qkv, band, out_weight, resid, modulation, up_weight, down_rows):
    dma = pltpu.SemaphoreType.DMA
    bf16 = jnp.bfloat16
    anywhere, vmem = pl.BlockSpec(memory_space=pl.ANY), pl.BlockSpec(memory_space=pltpu.VMEM)
    return pl.pallas_call(
        layer_kernel,
        out_shape=jax.ShapeDtypeStruct((ROWS, D), bf16),
        in_specs=[
            anywhere, pl.BlockSpec(memory_space=pltpu.SMEM), anywhere, anywhere, vmem, vmem, vmem,
        ],
        out_specs=vmem,
        scratch_shapes=[
            pltpu.VMEM((GROUP, 3, SLOTS, BLOCK, HD), bf16),
            pltpu.VMEM((GROUP, 2, BLOCK, HD), bf16),
            pltpu.VMEM((BLOCK, INNER), bf16),
            pltpu.VMEM((STREAMS, 4, 2, PART, D), bf16),
            pltpu.VMEM((2, 4, 4, WROWS, PACK), bf16),
            pltpu.VMEM((WROWS, PACK), bf16),
            pltpu.VMEM((STREAMS, 4, PART, D), bf16),
            pltpu.VMEM((STREAMS, 2, PART, HALF), bf16),
            pltpu.VMEM((STREAMS, 2, PART, D), bf16),
            pltpu.VMEM((STREAMS, PART, D), jnp.float32),
            pltpu.VMEM((ROWS, D), bf16),
            pltpu.VMEM((STREAMS, 8, 2, PART, D), bf16),
            pltpu.VMEM((16 * PART, 512), bf16),
            pltpu.VMEM((STREAMS * 16, PART, D), bf16),
            pltpu.VMEM((STREAMS, 8, PART, D), bf16),
            pltpu.VMEM((STREAMS, 2, 4, PART, D), bf16),
            dma((GROUP, N_HEAD - 1, 2)), dma((GROUP, N_HEAD - 1, 2)), dma((GROUP,)),
            dma((GROUP, 20)), dma((GROUP, SLOTS + 2)), dma,
            dma((1,)), dma((21,)), dma((21,)),
            dma((STREAMS, 4)), dma((STREAMS, 4)), dma((STREAMS, 4)), dma((STREAMS, 4)),
            dma((STREAMS, 2, 4, 2)), dma((STREAMS, 2, 4, 2)), dma((STREAMS, 9)), dma((STREAMS, 9)),
            dma((STREAMS, 8)), dma((STREAMS, 8)), dma((STREAMS, 2, 4, 2)), dma((STREAMS, 2, 4, 2)),
        ],
        compiler_params=pltpu.CompilerParams(
            collective_id=0, has_side_effects=True, vmem_limit_bytes=62 * MIB
        ),
        name="layer",
    )(qkv, band, out_weight, resid, modulation, up_weight, down_rows)


def shards(resid, qkv, band, out_weight, modulation, up_weight, down_weight):
    return layer(
        jnp.transpose(qkv, (1, 0, 2)), band, out_weight.reshape(INNER // PART, PART, D),
        resid, modulation, up_weight, jnp.transpose(down_weight),
    )


def solution(mesh):
    in_specs = (
        P("frame", None),
        P(("frame", "head"), None, None),
        P("frame", None),
        P("head", None),
        P(),
        P("frame", "head"),
        P("head", "frame"),
    )
    out_specs = P(("frame", "head"), None)
    return jax.shard_map(shards, mesh=mesh, in_specs=in_specs, out_specs=out_specs, check_vma=False)
```

```python
import functools
import math

import jax
import jax.numpy as jnp
from jax import lax
from jax.experimental import pallas as pl
from jax.experimental.pallas import tpu as pltpu
from jax.sharding import PartitionSpec as P

HD = 128
SLOTS = 9
BLOCK = 384
NBLK = 32
N_HEAD = 8
ROWS = BLOCK // N_HEAD
GROUP = 5
INNER = GROUP * HD
D = 5120
MESH = pl.DeviceIdType.MESH
MIB = 2**20

partner_offsets = (0, -8, -4, -2, -1, 1, 2, 4, 8)
VIA = "via"
SLOT = {offset: slot for slot, offset in enumerate(partner_offsets)}
QUERY_ROWS = 128
SCALE_LOG2 = math.log2(math.e) / math.sqrt(HD)
HALF = D // 2
UNITS = 432
MAIN = 384
TAIL = UNITS - MAIN
PACK = 896
WROWS = 160
STREAMS = 3
PART = ROWS // STREAMS
LAG = 2


def layer_kernel(
    qkv_ref, band_ref, out_weight_ref, resid_ref, modulation_ref, up_ref, down_rows_ref, out_ref,
    heads, via, attended, partial_ref,
    weights, other_pack, sib1, opposite, pairs, state, resid_rows, normed, hidden, down, sib2, ring,
    a2a_send, a2a_recv, own_sem, halo_send, halo_recv, weight_sem,
    local_sem, w_send, w_recv, s1_send, s1_recv, r1_send, r1_recv,
    ag_send, ag_recv, agsib_send, agsib_recv, s2_send, s2_recv, r2_send, r2_recv,
):
    me = lax.axis_index("head")
    frame = lax.axis_index("frame")
    block = frame
    z_hi, core = me // 2, lax.rem(me, 2)
    z_lo, yx = frame // 16, lax.rem(frame, 16)
    y, x = yx // 4, lax.rem(yx, 4)
    z = z_hi * 2 + z_lo
    row_start = frame - x
    halves = (pl.ds(0, HALF), pl.ds(HALF, HALF))

    def z_device(other):
        return {"head": (other // 2) * 2 + core, "frame": lax.rem(other, 2) * 16 + yx}

    sibling = {"head": z_hi * 2 + 1 - core, "frame": frame}
    above, below = z_device(lax.rem(z + 1, 8)), z_device(lax.rem(z + 7, 8))
    above2, below2 = z_device(lax.rem(z + 2, 8)), z_device(lax.rem(z + 6, 8))
    x_peers = [{"head": me, "frame": z_lo * 16 + y * 4 + lax.rem(x + k, 4)} for k in (1, 2, 3)]
    y_peers = [{"head": me, "frame": z_lo * 16 + lax.rem(y + k, 4) * 4 + x} for k in (1, 2, 3)]
    other_plane = z_device(z + 1 - 2 * z_lo)

    barrier = pltpu.get_barrier_semaphore()
    greeted = [above, below] + x_peers + y_peers
    greeted += [{"head": lax.rem(me + k, N_HEAD), "frame": frame} for k in range(1, N_HEAD)]
    greeted += [{"head": me, "frame": lax.rem(frame + k, NBLK)} for k in (4, 12, 16, 20, NBLK - 4)]
    for device in greeted:
        pl.semaphore_signal(barrier, inc=1, device_id=device, device_id_type=MESH)

    my_rows = pl.ds(pl.multiple_of(me * ROWS, 16), ROWS)
    fetch_resid = pltpu.make_async_copy(resid_ref.at[my_rows], resid_rows, local_sem.at[0])
    fetch_resid.start()

    lane = lax.broadcasted_iota(jnp.int32, (WROWS, 128), 1)
    blank = jnp.zeros((WROWS, 128 - 2 * TAIL), jnp.float32)
    tails = [
        jnp.concatenate([ref[:, 2 * MAIN:].astype(jnp.float32), blank], axis=1)
        for ref in (up_ref, down_rows_ref)
    ]
    up_tail = [tails[0], pltpu.roll(tails[0], 128 - TAIL, 1)]
    down_tail = [pltpu.roll(tails[1], TAIL, 1), tails[1]]
    mixed_tail = []
    for side in (0, 1):
        down_part = jnp.where(lane < 2 * TAIL, down_tail[side], 0.0)
        mixed_tail.append(jnp.where(lane < TAIL, up_tail[side], down_part))

    def pack(target, side):
        columns = pl.ds(pl.multiple_of(side * MAIN, 128), MAIN)
        target[:, 0:MAIN] = up_ref[:, columns]
        target[:, MAIN:512] = jnp.where(side == 0, mixed_tail[0], mixed_tail[1]).astype(jnp.bfloat16)
        target[:, 512:PACK] = down_rows_ref[:, columns]

    pack(other_pack, 1 - z_lo)
    pack(weights.at[z_lo, y, x], z_lo)

    pl.semaphore_wait(barrier, len(greeted))

    def remote(source, target, send_sem, recv_sem, device):
        return pltpu.make_async_remote_copy(
            source, target, send_sem, recv_sem, device_id=device, device_id_type=MESH
        )

    own_view, other_view = weights.at[z_lo, y, x], weights.at[1 - z_lo, y, x]
    cross = remote(other_pack, own_view, w_send.at[0], w_recv.at[0], other_plane)
    right, left = lax.rem(x + 1, 4), lax.rem(x + 3, 4)
    front, back = lax.rem(y + 1, 4), lax.rem(y + 3, 4)
    to_right, to_left, to_front, to_back = x_peers[0], x_peers[2], y_peers[0], y_peers[2]
    upper, lower = pl.ds(0, WROWS // 2), pl.ds(WROWS // 2, WROWS // 2)
    low, high = pl.ds(0, 2), pl.ds(2, 2)

    def weight_hops(first, hops):
        return [
            remote(view, view, w_send.at[first + i], w_recv.at[first + i], device)
            for i, (view, device) in enumerate(hops)
        ]

    def row_part(row, part):
        return weights.at[z_lo, row, part]

    def column_part(column, part):
        return weights.at[1 - z_lo, part, column]

    piece_near = weight_hops(1, (
        (own_view, to_right), (own_view, to_left), (other_view, to_front), (other_view, to_back),
    ))
    piece_far = weight_hops(5, (
        (weights.at[z_lo, y, left, upper], to_right), (weights.at[z_lo, y, right, lower], to_left),
        (weights.at[1 - z_lo, back, x, upper], to_front), (weights.at[1 - z_lo, front, x, lower], to_back),
    ))
    line_first = weight_hops(9, (
        (row_part(y, low), to_front), (row_part(y, high), to_back),
        (column_part(x, low), to_right), (column_part(x, high), to_left),
    ))
    line_then = weight_hops(13, (
        (row_part(y, high), to_front), (row_part(y, low), to_back),
        (column_part(x, high), to_right), (column_part(x, low), to_left),
    ))
    line_far = weight_hops(17, (
        (row_part(back, low), to_front), (row_part(front, high), to_back),
        (column_part(left, low), to_right), (column_part(right, high), to_left),
    ))
    weight_copies = [cross] + piece_near + piece_far + line_first + line_then + line_far

    def weight_step(landed, sent):
        for copy in landed:
            copy.wait_recv()
        for copy in sent:
            copy.start()

    def frame_device(frame):
        return {"head": me, "frame": frame}

    def head_device(head):
        return {"head": head, "frame": block}

    fetch_weight = pltpu.make_async_copy(out_weight_ref, down.at[0:INNER // PART], weight_sem)

    queries_part, halo_part = slice(0, 1), slice(1, 3)

    def to_peer(j, k, part):
        peer = lax.rem(me + k, N_HEAD)
        columns = pl.ds(pl.multiple_of(peer * INNER + j * HD, HD), HD)
        kind = part.start
        return pltpu.make_async_remote_copy(
            qkv_ref.at[part, :, columns], heads.at[j, part, 0, my_rows],
            a2a_send.at[j, k - 1, kind], a2a_recv.at[j, k - 1, kind],
            device_id=head_device(peer), device_id_type=MESH,
        )

    def wait_peers(j, part):
        for k in range(1, N_HEAD):
            origin = lax.rem(me + N_HEAD - k, N_HEAD)
            landed = heads.at[j, part, 0, pl.ds(pl.multiple_of(origin * ROWS, 16), ROWS)]
            pltpu.make_async_copy(landed, landed, a2a_recv.at[j, k - 1, part.start]).wait()

    def own_piece(j):
        columns = pl.ds(pl.multiple_of(me * INNER + j * HD, HD), HD)
        return pltpu.make_async_copy(
            qkv_ref.at[:, :, columns], heads.at[j, :, 0, my_rows], own_sem.at[j]
        )

    def send_heads(j, carry):
        for k in (4, 3, 5, 2, 6, 1, 7):
            to_peer(j, k, halo_part).start()
        own_piece(j).start()
        return carry

    def send_queries(j):
        for k in (4, 3, 5, 2, 6, 1, 7):
            to_peer(j, k, queries_part).start()

    lax.fori_loop(0, 2, send_heads, 0)
    for copy in piece_near[:2]:
        copy.start()
    fetch_weight.start()

    low4, high4 = block >= 4, block < NBLK - 4
    both, keys_only, values_only = slice(1, 3), slice(1, 2), slice(2, 3)
    routes = (
        (1, 0, -4, block + 4, high4, both),
        (1, 0, 4, block - 4, low4, both),
        (1, 0, -1, block + 1, x < 3, both),
        (1, 0, 1, block - 1, x > 0, both),
        (2, -4, -8, block + 4, low4 & high4 & (block // 4 != 3), both),
        (2, 4, 8, block - 4, low4 & high4 & (block // 4 != 4), both),
        (2, -4, VIA, block - 12, block // 4 == 3, both),
        (2, 4, VIA, block + 12, block // 4 == 4, both),
        (3, VIA, -8, block + 16, block // 4 == 0, both),
        (3, VIA, 8, block - 16, block // 4 == 7, both),
        (2, -4, -1, row_start, (x == 3) & low4, both),
        (2, 4, 1, row_start + 3, (x == 0) & high4, both),
        (2, -1, -2, block + 1, (x == 1) | (x == 2), both),
        (2, 1, 2, block - 1, (x == 1) | (x == 2), both),
        (2, -4, -2, row_start, (x == 2) & low4, keys_only),
        (2, 4, 2, row_start + 3, (x == 1) & high4, keys_only),
        (3, -1, -2, block + 1, (x == 0) & low4, both),
        (3, 1, 2, block - 1, (x == 3) & high4, both),
        (3, 2, -2, block + 4, (x == 0) & high4, values_only),
        (3, -2, 2, block - 4, (x == 3) & low4, values_only),
    )
    arrivals = (
        (2, -4, low4, both),
        (2, 4, high4, both),
        (2, -1, x > 0, both),
        (2, 1, x < 3, both),
        (3, VIA, (block // 4 == 0) | (block // 4 == 7), both),
        (3, -1, (x == 0) & low4, both),
        (3, 1, (x == 3) & high4, both),
        (3, 2, x == 0, both),
        (3, -2, x == 3, both),
        (4, 2, (x != 0) & (x != 3) & (block < NBLK - 2), both),
        (4, -2, (x != 0) & (x != 3) & (block >= 2), both),
        (4, -2, (x == 0) & low4, keys_only),
        (4, -2, (x == 0) & low4, values_only),
        (4, 2, (x == 3) & high4, keys_only),
        (4, 2, (x == 3) & high4, values_only),
        (4, -8, block >= 8, both),
        (4, 8, block < NBLK - 8, both),
    )

    def place(j, slot, part):
        return via.at[j] if slot == VIA else heads.at[j, part, SLOT[slot]]

    def halo_sem(slot, part):
        if part is values_only:
            return SLOTS + (slot > 0)
        return SLOTS - 1 if slot == VIA else SLOT[slot] - 1

    def route_copy(j, index):
        _, source, target, frame_to, _, part = routes[index]
        return pltpu.make_async_remote_copy(
            place(j, source, part), place(j, target, part),
            halo_send.at[j, index], halo_recv.at[j, halo_sem(target, part)],
            device_id=frame_device(jnp.clip(frame_to, 0, NBLK - 1)), device_id_type=MESH,
        )

    def send_stage(j, stage):
        for index, route in enumerate(routes):
            if route[0] == stage:
                @pl.when(route[4])
                def _():
                    route_copy(j, index).start()

    def wait_stage(j, stage):
        for before, slot, when, part in arrivals:
            if before == stage:
                @pl.when(when)
                def _():
                    landed = place(j, slot, part)
                    pltpu.make_async_copy(landed, landed, halo_recv.at[j, halo_sem(slot, part)]).wait()

    for offset in partner_offsets[1:]:
        partner = block + offset

        @pl.when((partner < 0) | (partner >= NBLK))
        def _():
            heads[:, 1:3, SLOT[offset]] = jnp.zeros((GROUP, 2, BLOCK, HD), jnp.bfloat16)

    def attend(j):
        widths = []
        for slot, offset in enumerate(partner_offsets):
            partner = block + offset
            present = (partner >= 0) & (partner < NBLK)
            widths.append(jnp.where(present, band_ref[0, slot], 0))
        keys = heads[j, 1].reshape(SLOTS * BLOCK, HD)
        values = heads[j, 2].reshape(SLOTS * BLOCK, HD)
        columns = pl.ds(pl.multiple_of(j * HD, HD), HD)
        for first in range(0, BLOCK, QUERY_ROWS):
            queries = heads[j, 0, 0, first:first + QUERY_ROWS]
            scores = lax.dot_general(
                queries, keys, (((1,), (1,)), ((), ())), preferred_element_type=jnp.float32
            )
            row = lax.broadcasted_iota(jnp.int32, (QUERY_ROWS, BLOCK), 0) + first
            column = lax.broadcasted_iota(jnp.int32, (QUERY_ROWS, BLOCK), 1)
            distance = jnp.abs(row - column)
            parts = []
            for slot in range(SLOTS):
                part = scores[:, slot * BLOCK:(slot + 1) * BLOCK]
                parts.append(jnp.where(distance < widths[slot], part, -1e30))
            top = functools.reduce(jnp.maximum, parts)
            row_max = jnp.max(top, axis=1, keepdims=True)
            weights = [jnp.exp2((part - row_max) * SCALE_LOG2) for part in parts]
            denominator = jnp.sum(functools.reduce(jnp.add, weights), axis=1, keepdims=True)
            probabilities = jnp.concatenate([w.astype(jnp.bfloat16) for w in weights], axis=1)
            summed = jnp.dot(probabilities, values, preferred_element_type=jnp.float32)
            attended[first:first + QUERY_ROWS, columns] = (summed / denominator).astype(jnp.bfloat16)

    def step(it, carry):
        @pl.when(it < GROUP)
        def _():
            wait_peers(it, halo_part)
            own_piece(it).wait()
            send_stage(it, 1)

        @pl.when(it < GROUP - 2)
        def _():
            send_heads(it + 2, 0)

        @pl.when(it < GROUP)
        def _():
            send_queries(it)

        @pl.when((it >= 1) & (it < GROUP + 1))
        def _():
            wait_stage(it - 1, 2)
            send_stage(it - 1, 2)

        @pl.when((it >= 2) & (it < GROUP + 2))
        def _():
            wait_stage(it - 2, 3)
            send_stage(it - 2, 3)

        @pl.when(it == 1)
        def _():
            weight_step([], [cross])

        @pl.when(it == 3)
        def _():
            weight_step([cross], piece_near[2:])

        @pl.when(it == GROUP)
        def _():
            weight_step(piece_near, piece_far)

        @pl.when(it == GROUP + 2)
        def _():
            weight_step(piece_far, [])

        @pl.when(it >= 3)
        def _():
            wait_peers(it - 3, queries_part)
            wait_stage(it - 3, 4)
            attend(it - 3)

        return carry

    lax.fori_loop(0, GROUP + 3, step, 0)

    fetch_weight.wait()

    started = []

    def send(source, target, send_sem, recv_sem, device):
        copy = pltpu.make_async_remote_copy(
            source, target, send_sem, recv_sem, device_id=device, device_id_type=MESH
        )
        copy.start()
        started.append(copy)
        return copy

    order = [lax.rem(z_hi + k, 4) for k in (2, 1, 3, 0)]
    parts = [slice(r * PART, (r + 1) * PART) for r in range(STREAMS)]
    s1 = []

    def project_heads(r):
        rows = attended[...].reshape(N_HEAD, STREAMS, PART, INNER)[:, r].reshape(N_HEAD * PART, INNER)

        def columns_of(c, carry):
            columns = pl.ds(pl.multiple_of(c * 512, 512), 512)
            weight = down[0:INNER // PART, :, columns].reshape(INNER, 512)
            product = jnp.dot(rows, weight, preferred_element_type=jnp.float32)
            partial_ref[r, :, :, :, columns] = product.astype(jnp.bfloat16).reshape(4, 2, PART, 512)
            return carry

        lax.fori_loop(0, D // 512, columns_of, 0)
        s1.append([
            send(
                partial_ref.at[r, q, 1 - core], sib1.at[r, q],
                s1_send.at[r, i], s1_recv.at[r, i], sibling,
            )
            for i, q in enumerate(order)
        ])

    def shard(distance):
        return lax.rem(z + distance + 8, 8)

    def up(r):
        rows = normed[r].reshape(16 * PART, D)
        total = None
        for c in range(4):
            weight = weights[c // 2, 2 * (c % 2):2 * (c % 2) + 2, :, :, 0:512].reshape(8 * WROWS, 512)
            product = jnp.dot(
                rows[:, c * 1280:(c + 1) * 1280], weight, preferred_element_type=jnp.float32
            )
            total = product if total is None else total + product
        active = jax.nn.gelu(total, approximate=True)
        place = lax.broadcasted_iota(jnp.int32, (16 * PART, 128), 1)
        tail = pltpu.roll(active[:, MAIN:512], TAIL, 1)
        tail = jnp.where((place >= TAIL) & (place < 2 * TAIL), tail, 0.0)
        hidden[:, 0:128] = tail.astype(jnp.bfloat16)
        hidden[:, 128:512] = active[:, 0:MAIN].astype(jnp.bfloat16)

    def project(r):
        def columns_of(c, carry):
            weight = weights[c // 4, lax.rem(c, 4), :, :, MAIN:PACK].reshape(4 * WROWS, 512)
            columns = pl.ds(pl.multiple_of(c * 4 * WROWS, 128), 4 * WROWS)
            product = lax.dot_general(
                hidden[...], weight, (((1,), (1,)), ((), ())), preferred_element_type=jnp.float32
            )
            down[r * 16:(r + 1) * 16, :, columns] = product.astype(jnp.bfloat16).reshape(16, PART, 4 * WROWS)
            return carry

        lax.fori_loop(0, 8, columns_of, 0)

    def stream(r):
        rows = parts[r]

        def pair(q):
            return partial_ref[r, q, core].astype(jnp.float32) + sib1[r, q].astype(jnp.float32)

        s1[r][0].wait_recv()
        q = order[0]
        sib1[r, q] = pair(q).astype(jnp.bfloat16)
        opposites = [
            send(
                sib1.at[r, q, :, halves[way]], opposite.at[r, way],
                r1_send.at[r, way], r1_recv.at[r, way], (above2, below2)[way],
            )
            for way in (0, 1)
        ]
        yield
        finals = []
        for way in (0, 1):
            s1[r][1 + way].wait_recv()
            opposites[way].wait_recv()
            q = order[1 + way]
            total = pair(q)
            moved = total[:, way * HALF:(way + 1) * HALF] + opposite[r, way].astype(jnp.float32)
            kept = total[:, (1 - way) * HALF:(2 - way) * HALF]
            sib1[r, q, :, halves[way]] = moved.astype(jnp.bfloat16)
            sib1[r, q, :, halves[1 - way]] = kept.astype(jnp.bfloat16)
            finals.append(send(
                sib1.at[r, q], pairs.at[r, way],
                r1_send.at[r, 2 + way], r1_recv.at[r, 2 + way], (above2, below2)[way],
            ))
        yield
        s1[r][3].wait_recv()
        for copy in finals:
            copy.wait_recv()
        if r == 0:
            fetch_resid.wait()
        branch = (
            pair(z_hi) + pairs[r, 0].astype(jnp.float32) + pairs[r, 1].astype(jnp.float32)
        )
        value = resid_rows[rows].astype(jnp.float32) + modulation_ref[0:1] * branch
        state[r] = value
        average = jnp.mean(value, axis=-1, keepdims=True)
        centered = value - average
        variance = jnp.mean(centered * centered, axis=-1, keepdims=True)
        normal_form = centered * lax.rsqrt(variance + 1e-06)
        normed[r, z, core] = (
            normal_form * (1.0 + modulation_ref[2:3]) + modulation_ref[1:2]
        ).astype(jnp.bfloat16)

        gathered = []

        def to_sibling(view, index):
            gathered.append(send(
                view, view, agsib_send.at[r, index], agsib_recv.at[r, index], sibling
            ))

        hops = {}

        def hop(way, step, half):
            view = normed.at[r, shard((1 - step) * (1 - 2 * way)), core, :, halves[half]]
            hops[way, half] = send(
                view, view, ag_send.at[r, way, step - 1, half], ag_recv.at[r, way, step - 1, half],
                (above, below)[way],
            )

        for half in (0, 1):
            for way in (0, 1):
                hop(way, 1, half)
        to_sibling(normed.at[r, z, core], 0)
        yield
        for step in (1, 2, 3, 4):
            for half in (0, 1):
                for way in (0, 1):
                    if step < 4 or half == way:
                        hops[way, half].wait_recv()
                    if step < 3 or step == 3 and half == way:
                        hop(way, step + 1, half)
            for way in (0, 1):
                view = normed.at[r, shard(-step * (1 - 2 * way)), core]
                if step == 4:
                    view = view.at[:, halves[way]]
                to_sibling(view, 1 + (step - 1) * 2 + way)
            yield
        for copy in gathered:
            copy.wait_recv()
        if r == 0:
            weight_step(line_then + line_far, [])
        up(r)
        project(r)
        s2 = {}
        for i, distance in enumerate((4, 3, -3, 2, -2, 1, -1, 0)):
            q = shard(distance)
            s2[distance] = send(
                down.at[r * 16 + q * 2 + 1 - core], sib2.at[r, q], s2_send.at[r, i], s2_recv.at[r, i], sibling
            )
        yield

        def pair2(q, columns):
            return (
                down[r * 16 + q * 2 + core, :, columns].astype(jnp.float32)
                + sib2[r, q, :, columns].astype(jnp.float32)
            )

        sums = {}
        for step in (1, 2, 3, 4):
            for way in (0, 1):
                if step > 1:
                    s2[(5 - step) * (1 - 2 * way)].wait_recv()
                elif way == 0:
                    s2[4].wait_recv()
            for turn in (0, 1):
                for way in (0, 1):
                    half = way if turn else 1 - way
                    if step == 1 and not turn:
                        continue
                    q, columns = shard((5 - step) * (1 - 2 * way)), halves[half]
                    total = pair2(q, columns)
                    if (way, half) in sums:
                        sums[way, half].wait_recv()
                        total = total + ring[r, way, step - 2, :, columns].astype(jnp.float32)
                    sib2[r, q, :, columns] = total.astype(jnp.bfloat16)
                    sums[way, half] = send(
                        sib2.at[r, q, :, columns], ring.at[r, way, step - 1, :, columns],
                        r2_send.at[r, way, step - 1, half], r2_recv.at[r, way, step - 1, half],
                        (above, below)[way],
                    )
            yield
        s2[0].wait_recv()
        for half in (0, 1):
            columns = halves[half]
            ffn = pair2(z, columns)
            for way in (0, 1):
                sums[way, half].wait_recv()
                ffn = ffn + ring[r, way, 3, :, columns].astype(jnp.float32)
            out_ref[rows, columns] = (
                state[r, :, columns] + modulation_ref[3:4, columns] * ffn
            ).astype(jnp.bfloat16)
        yield

    stages = 13
    streams = [stream(r) for r in range(STREAMS)]
    project_heads(0)
    project_heads(1)
    weight_step([], line_first + line_then)
    for tick in range(stages + LAG * (STREAMS - 1)):
        for r in range(STREAMS):
            if 0 <= tick - LAG * r < stages:
                next(streams[r])
        if tick == 0:
            project_heads(2)
        if tick == 2:
            weight_step(line_first, line_far)

    for copy in started + weight_copies:
        copy.wait_send()
    def finish(j, carry):
        for k in range(1, N_HEAD):
            to_peer(j, k, queries_part).wait_send()
            to_peer(j, k, halo_part).wait_send()
        for index, route in enumerate(routes):
            @pl.when(route[4])
            def _():
                route_copy(j, index).wait_send()
        return carry

    lax.fori_loop(0, GROUP, finish, 0)


def layer(qkv, band, out_weight, resid, modulation, up_weight, down_rows):
    dma = pltpu.SemaphoreType.DMA
    bf16 = jnp.bfloat16
    anywhere, vmem = pl.BlockSpec(memory_space=pl.ANY), pl.BlockSpec(memory_space=pltpu.VMEM)
    return pl.pallas_call(
        layer_kernel,
        out_shape=jax.ShapeDtypeStruct((ROWS, D), bf16),
        in_specs=[
            anywhere, pl.BlockSpec(memory_space=pltpu.SMEM), anywhere, anywhere, vmem, vmem, vmem,
        ],
        out_specs=vmem,
        scratch_shapes=[
            pltpu.VMEM((GROUP, 3, SLOTS, BLOCK, HD), bf16),
            pltpu.VMEM((GROUP, 2, BLOCK, HD), bf16),
            pltpu.VMEM((BLOCK, INNER), bf16),
            pltpu.VMEM((STREAMS, 4, 2, PART, D), bf16),
            pltpu.VMEM((2, 4, 4, WROWS, PACK), bf16),
            pltpu.VMEM((WROWS, PACK), bf16),
            pltpu.VMEM((STREAMS, 4, PART, D), bf16),
            pltpu.VMEM((STREAMS, 2, PART, HALF), bf16),
            pltpu.VMEM((STREAMS, 2, PART, D), bf16),
            pltpu.VMEM((STREAMS, PART, D), jnp.float32),
            pltpu.VMEM((ROWS, D), bf16),
            pltpu.VMEM((STREAMS, 8, 2, PART, D), bf16),
            pltpu.VMEM((16 * PART, 512), bf16),
            pltpu.VMEM((STREAMS * 16, PART, D), bf16),
            pltpu.VMEM((STREAMS, 8, PART, D), bf16),
            pltpu.VMEM((STREAMS, 2, 4, PART, D), bf16),
            dma((GROUP, N_HEAD - 1, 2)), dma((GROUP, N_HEAD - 1, 2)), dma((GROUP,)),
            dma((GROUP, 20)), dma((GROUP, SLOTS + 2)), dma,
            dma((1,)), dma((21,)), dma((21,)),
            dma((STREAMS, 4)), dma((STREAMS, 4)), dma((STREAMS, 4)), dma((STREAMS, 4)),
            dma((STREAMS, 2, 4, 2)), dma((STREAMS, 2, 4, 2)), dma((STREAMS, 9)), dma((STREAMS, 9)),
            dma((STREAMS, 8)), dma((STREAMS, 8)), dma((STREAMS, 2, 4, 2)), dma((STREAMS, 2, 4, 2)),
        ],
        compiler_params=pltpu.CompilerParams(
            collective_id=0, has_side_effects=True, vmem_limit_bytes=62 * MIB
        ),
        name="layer",
    )(qkv, band, out_weight, resid, modulation, up_weight, down_rows)


def shards(resid, qkv, band, out_weight, modulation, up_weight, down_weight):
    return layer(
        jnp.transpose(qkv, (1, 0, 2)), band, out_weight.reshape(INNER // PART, PART, D),
        resid, modulation, up_weight, jnp.transpose(down_weight),
    )


def solution(mesh):
    in_specs = (
        P("frame", None),
        P(("frame", "head"), None, None),
        P("frame", None),
        P("head", None),
        P(),
        P("frame", "head"),
        P("head", "frame"),
    )
    out_specs = P(("frame", "head"), None)
    return jax.shard_map(shards, mesh=mesh, in_specs=in_specs, out_specs=out_specs, check_vma=False)
```
